256 devices in a mesh: row: 8 (over y, core), col: 32 (over z, x).
Axes of the slice: x: 4, y: 4, z: 8, core: 2. Of those that a mesh axis runs over, the one named last changes fastest.
Arguments:
- panel: float32 [16384, 256], P(('row', 'col')), may hold values from -7 to 7, as said below
- trailing: float32 [16384, 16384], P('row', 'col'), may hold values from -5 to 5
- vectors: float32 [16384, 512], P('row', 'col'), may hold values from -6 to 6
Outputs:
- band_block: float32 [256, 256], replicated
- updated: float32 [16384, 16384], P('row', 'col')
- rotated: float32 [16384, 512], P('row', 'col')
The draws below stay inside these ranges and needn't reach their ends.
Inputs may be any that keep to these rules, and one draw needn't show every extreme that they name: panel has full column rank.
All inputs are finite; a program needn't handle non-finite values.
Results may differ from the reference program's by a relative error of at most 0.00007.
Values sent between devices are 32-bit elements; how exact they have to be, the bound alone decides.
No kernel may reach another device: no remote copies, remote signals or barrier semaphores. Data moves between devices by JAX's collectives and lax.ppermute only.
A program may use at most 64 MiB of HBM per device.

```python
import math
import jax
import jax.numpy as jnp
from jax import lax

M = 16384
B = 256
EIG = 512


def draw_panel(key, part):
    key = jax.random.fold_in(key, 1)
    key_base, key_cols, key_rows = jax.random.split(key, 3)
    base = jnp.clip(jax.random.normal(key_base, (M, B), jnp.float32), -5.0, 5.0)
    col_scales = jnp.exp(jax.random.uniform(key_cols, (1, B), jnp.float32) * math.log(10.0))
    row_scales = jnp.exp(jax.random.uniform(key_rows, (M, 1), jnp.float32) * math.log(3.0))
    return base * col_scales * row_scales / math.sqrt(M)


def draw_trailing(key, part):
    key = jax.random.fold_in(key, 2)
    base = jnp.clip(jax.random.normal(key, (M, M), jnp.float32), -5.0, 5.0)
    return 0.5 * (base + base.T)


def level_of(own_key, dims, cuts, low, top_value):
    def one(axis_at, parts):
        draws = jax.random.uniform(jax.random.fold_in(jax.random.fold_in(own_key, 6), axis_at), (parts,), jnp.float32, low / len(cuts), top_value / len(cuts))
        return jnp.repeat(jnp.exp(draws), dims[axis_at] // parts).reshape((-1,) + (1,) * (len(dims) - axis_at - 1))

    level = one(*cuts[0])
    for cut in cuts[1:]:
        level = level * one(*cut)
    return level


def bell_draw(rng, extent, deviation, reach, shards=(), kind=jnp.bfloat16):
    drawn = deviation * jax.random.normal(rng, extent, jnp.float32)
    if shards:
        drawn = drawn * level_of(rng, extent, shards, -0.22, 0.18)
    return jnp.clip(drawn, -reach, reach).astype(kind)


def setup_inputs(seed: int = 0) -> dict:
    key_of = jax.random.split(jax.random.key(seed), 4)
    panel = draw_panel(jax.random.fold_in(key_of[3], 71), 0)
    trailing = draw_trailing(jax.random.fold_in(key_of[3], 71), 0)
    vectors = bell_draw(key_of[2], (M, EIG), 1.0, 6.0, ((0, 8), (1, 32)), jnp.float32)
    return {"panel": panel, "trailing": trailing, "vectors": vectors}


def exact_dot(left, right):
    return jnp.dot(left.astype(jnp.float32), right.astype(jnp.float32), precision=lax.Precision.HIGHEST, preferred_element_type=jnp.float32)

def reference(panel, trailing, vectors):
    gram_matrix = exact_dot(panel.T, panel)
    lower = jnp.linalg.cholesky(gram_matrix)
    upper_factor = lower.T
    basis = lax.linalg.triangular_solve(lower, panel, left_side=False, lower=True, transpose_a=True)
    product = exact_dot(trailing, basis)
    coupling = exact_dot(basis.T, product)
    zeta = 2.0 * product - 2.0 * exact_dot(basis, coupling)
    left_factors = jnp.concatenate([basis, zeta], axis=1)
    right_factors = jnp.concatenate([zeta, basis], axis=1)
    updated = trailing - lax.dot_general(left_factors.astype(jnp.float32), right_factors.astype(jnp.float32), (((1,), (1,)), ((), ())), precision=lax.Precision.HIGHEST, preferred_element_type=jnp.float32)
    projected = exact_dot(basis.T, vectors)
    rotated = vectors - 2.0 * exact_dot(basis, projected)
    return (upper_factor, updated, rotated)
```

```python
import jax
import jax.numpy as jnp
from jax import lax
from jax.sharding import Mesh, PartitionSpec as P

EXACT = lax.Precision.HIGHEST
CLOSE = lax.Precision.HIGH


def dot(left, right, dims=((1,), (0,)), precision=EXACT):
    return lax.dot_general(
        left, right, (dims, ((), ())), precision=precision, preferred_element_type=jnp.float32
    )


def shift(x, axis, step):
    n = lax.axis_size(axis)
    return lax.ppermute(x, axis, [(i, (i + step) % n) for i in range(n)])


def gather_z(x):
    n = lax.axis_size("z")
    return lax.all_to_all(jnp.broadcast_to(x[None], (n,) + x.shape), "z", 0, 0)


def gather_x(x):
    half = x.shape[0] // 2
    from_low = shift(x, "x", 1)
    from_high = shift(x, "x", -1)
    far_a = shift(from_low[:half], "x", 1)
    far_b = shift(from_high[half:], "x", -1)
    far = jnp.concatenate([far_a, far_b], axis=0)
    own = lax.axis_index("x")
    out = jnp.zeros((4,) + x.shape, x.dtype)
    for offset, piece in enumerate((x, from_high, far, from_low)):
        out = lax.dynamic_update_index_in_dim(out, piece, (own + offset) % 4, 0)
    return out


def gather_col(x):
    pieces = gather_x(gather_z(x))
    return pieces.transpose(1, 0, 2, 3).reshape(-1, x.shape[1])


def scatter_row(x):
    core, y = lax.axis_index("core"), lax.axis_index("y")
    pairs = x.reshape((4, 2) + x.shape[1:])
    mine = lax.dynamic_index_in_dim(pairs, core, 1, keepdims=False)
    other = lax.dynamic_index_in_dim(pairs, 1 - core, 1, keepdims=False)
    part = mine + lax.ppermute(other, "core", [(0, 1), (1, 0)])
    total = lax.dynamic_index_in_dim(part, y, 0, keepdims=False)
    for step in (1, 2, 3):
        piece = lax.dynamic_index_in_dim(part, (y + step) % 4, 0, keepdims=False)
        total = total + shift(piece, "y", step)
    return total


def sum_row(x):
    x = x + lax.ppermute(x, "core", [(0, 1), (1, 0)])
    x = x + lax.ppermute(x, "y", [(i, i ^ 1) for i in range(4)])
    return x + lax.ppermute(x, "y", [(i, i ^ 3) for i in range(4)])


def shards(panel, trailing, vectors):
    rows, width = panel.shape
    eig = vectors.shape[1]
    row, col = lax.axis_size(("y", "core")), lax.axis_size(("z", "x"))
    everywhere = ("y", "core", "z", "x")
    by_cols = [(c * row + r, r * col + c) for r in range(row) for c in range(col)]
    by_rows = [(b, a) for a, b in by_cols]

    col_panel = lax.all_gather(
        lax.ppermute(panel, everywhere, by_cols), ("y", "core"), axis=0, tiled=True
    )
    row_panel = gather_col(panel)

    part_product = dot(trailing, row_panel, ((0,), (0,)), CLOSE)
    part_gram = dot(row_panel, row_panel, ((0,), (0,)))
    part_projected = dot(vectors, row_panel, ((0,), (0,)))
    part_projected = jnp.pad(part_projected.reshape(row, -1, width), ((0, 0), (0, 8 - eig // row), (0, 0)))
    parts = jnp.concatenate(
        [part_product.reshape(row, -1, width), part_gram.reshape(row, -1, width), part_projected], axis=1
    )
    piece = scatter_row(parts)
    whole = lax.all_gather(piece, ("y", "core"), axis=0)
    gram_rows = width // row
    col_product = whole[:, :rows].reshape(-1, width)
    gram_matrix = whole[:, rows : rows + gram_rows].reshape(width, width)
    projected = whole[:, rows + gram_rows : rows + gram_rows + eig // row].reshape(eig, width)

    row_product = gather_col(lax.ppermute(piece[:rows], everywhere, by_rows))

    lower = jnp.linalg.cholesky(gram_matrix)
    inverse = lax.linalg.triangular_solve(
        lower, jnp.eye(width, dtype=jnp.float32), left_side=True, lower=True
    )
    row_basis = dot(row_panel, inverse, ((1,), (1,)))
    col_basis = dot(col_panel, inverse, ((1,), (1,)))

    middle = sum_row(dot(row_panel, row_product, ((0,), (0,))))
    coupling = dot(inverse, dot(middle, inverse, ((1,), (1,))))
    left = jnp.concatenate([row_basis, row_product], axis=1)
    right = jnp.concatenate(
        [
            2.0 * dot(col_product, inverse, ((1,), (1,))) - 2.0 * dot(col_basis, coupling + coupling.T),
            2.0 * dot(col_basis, inverse),
        ],
        axis=1,
    )
    updated = trailing - dot(left, right, ((1,), (1,)), CLOSE)
    rotated = vectors - 2.0 * dot(row_basis, dot(inverse, projected, ((1,), (1,))))
    return (lower.T, updated, rotated)


def solution(mesh):
    fine = Mesh(mesh.devices.reshape(4, 2, 8, 4), ("y", "core", "z", "x"))
    row, col = ("y", "core"), ("z", "x")
    return jax.shard_map(
        shards,
        mesh=fine,
        in_specs=(P(row + col, None), P(row, col), P(row, col)),
        out_specs=(P(), P(row, col), P(row, col)),
        check_vma=False,
    )
```

```python
import functools
import jax
import jax.numpy as jnp
from jax import lax
from jax.experimental import pallas as pl
from jax.experimental.pallas import tpu as pltpu
from jax.sharding import Mesh, PartitionSpec as P

EXACT = lax.Precision.HIGHEST
CLOSE = lax.Precision.HIGH
BLOCK = 64


def dot(left, right, dims=((1,), (0,)), precision=EXACT):
    return lax.dot_general(
        left, right, (dims, ((), ())), precision=precision, preferred_element_type=jnp.float32
    )


def factor_kernel(gram_ref, upper_ref, inverse_ref, work):
    n = gram_ref.shape[0]
    half = n // 2
    lane = lax.broadcasted_iota(jnp.int32, (8, half), 1)
    sub = lax.broadcasted_iota(jnp.int32, (8, half), 0)
    work[...] = gram_ref[...]
    for base in range(0, n, BLOCK):
        rest = base + BLOCK
        tiles = [
            [work[base + t : base + t + 8, h * half : (h + 1) * half] for h in (0, 1)]
            for t in range(0, BLOCK, 8)
        ]
        for j in range(BLOCK):
            side, at = (base + j) // half, (base + j) % half
            own, s = j // 8, j % 8
            scale = lax.rsqrt(tiles[own][side][s : s + 1, at : at + 1])
            pivot = [tiles[own][h][s : s + 1, :] * scale for h in (0, 1)]
            pivot[side] = jnp.where(lane[:1] == at, scale, pivot[side])
            for t in range(own, BLOCK // 8):
                weight = tiles[t][side][:, at : at + 1] * scale
                for h in (0, 1):
                    old = tiles[t][h]
                    kept = jnp.where(lane == at, 0.0, old) if h == side else old
                    new = kept - weight * pivot[h]
                    if t == own:
                        new = jnp.where(sub > s, new, jnp.where(sub == s, pivot[h], old))
                    tiles[t][h] = new
        rows = jnp.concatenate([jnp.concatenate(t, axis=1) for t in tiles], axis=0)
        wide = lax.broadcasted_iota(jnp.int32, (BLOCK, n), 1)
        tall = lax.broadcasted_iota(jnp.int32, (BLOCK, n), 0) + base
        upper_ref[base:rest, :] = jnp.where(
            wide > tall, rows, jnp.where(wide == tall, 1.0 / rows, 0.0)
        )
        inverse_ref[base:rest, :] = jnp.where(wide <= tall, rows, 0.0)
        if rest < n:
            lower_rows = jnp.where((wide > tall) & (wide < rest), 0.0, rows)
            change = dot(rows, lower_rows, ((0,), (0,)))
            wide = lax.broadcasted_iota(jnp.int32, (n - rest, n), 1)
            below = jnp.where((wide >= base) & (wide < rest), 0.0, work[rest:, :])
            work[rest:, :] = below - change[rest:, :]


def factor(gram):
    n = gram.shape[0]
    shape = jax.ShapeDtypeStruct((n, n), jnp.float32)
    return pl.pallas_call(
        factor_kernel,
        out_shape=(shape, shape),
        scratch_shapes=[pltpu.VMEM((n, n), jnp.float32)],
        cost_estimate=pl.CostEstimate(
            flops=20_000_000_000, bytes_accessed=12 * n * n, transcendentals=n
        ),
    )(gram)


def shift(x, axis, step):
    n = lax.axis_size(axis)
    return lax.ppermute(x, axis, [(i, (i + step) % n) for i in range(n)])


def gather(x, axis):
    n = lax.axis_size(axis)
    return lax.all_to_all(jnp.broadcast_to(x[None], (n,) + x.shape), axis, 0, 0)


def gather_x(x):
    half = x.shape[0] // 2
    from_low = shift(x, "x", 1)
    from_high = shift(x, "x", -1)
    far_a = shift(from_low[:half], "x", 1)
    far_b = shift(from_high[half:], "x", -1)
    far = jnp.concatenate([far_a, far_b], axis=0)
    own = lax.axis_index("x")
    out = jnp.zeros((4,) + x.shape, x.dtype)
    for offset, piece in enumerate((x, from_high, far, from_low)):
        out = lax.dynamic_update_index_in_dim(out, piece, (own + offset) % 4, 0)
    return out


def scatter_row(x):
    core, y = lax.axis_index("core"), lax.axis_index("y")
    pairs = x.reshape((4, 2) + x.shape[1:])
    mine = lax.dynamic_index_in_dim(pairs, core, 1, keepdims=False)
    other = lax.dynamic_index_in_dim(pairs, 1 - core, 1, keepdims=False)
    part = mine + lax.ppermute(other, "core", [(0, 1), (1, 0)])
    total = lax.dynamic_index_in_dim(part, y, 0, keepdims=False)
    for step in (1, 2, 3):
        piece = lax.dynamic_index_in_dim(part, (y + step) % 4, 0, keepdims=False)
        total = total + shift(piece, "y", step)
    return total


def shards(panel, trailing, vectors):
    rows, width = panel.shape
    eig = vectors.shape[1]
    row, col = lax.axis_size(("y", "core")), lax.axis_size(("z", "x"))
    slab = width // row
    everywhere = ("y", "core", "z", "x")
    by_cols = [(c * row + r, r * col + c) for r in range(row) for c in range(col)]
    by_rows = [(b, a) for a, b in by_cols]

    col_panel = gather(lax.ppermute(panel, everywhere, by_cols), ("y", "core")).reshape(-1, width)
    pieces = gather_x(gather(panel, "z"))
    row_panel = pieces.transpose(1, 0, 2, 3).reshape(-1, width)

    part_product = dot(trailing, row_panel, ((0,), (0,)), CLOSE)
    part_middle = dot(col_panel, part_product, ((0,), (0,)))
    part_gram = dot(row_panel, row_panel, ((0,), (0,)))
    part_projected = dot(vectors, row_panel, ((0,), (0,)))
    part_projected = jnp.pad(part_projected.reshape(row, -1, width), ((0, 0), (0, 8 - eig // row), (0, 0)))
    parts = jnp.concatenate(
        [
            part_product.reshape(row, -1, width),
            part_middle.reshape(row, -1, width),
            part_gram.reshape(row, -1, width),
            part_projected,
        ],
        axis=1,
    )
    piece = scatter_row(parts)
    product_piece, middle_piece = piece[:rows], piece[rows : rows + slab]

    small = gather(piece[rows + slab :], ("y", "core"))
    gram_matrix = small[:, :slab].reshape(width, width)
    projected = small[:, slab : slab + eig // row].reshape(eig, width)
    col_product = gather(product_piece, ("y", "core")).reshape(-1, width)

    moved = jnp.concatenate([lax.ppermute(product_piece, everywhere, by_rows), middle_piece], axis=0)
    moved = gather(moved, "z")
    moved = jnp.concatenate(
        [moved[:, :rows].reshape(-1, width), jnp.sum(moved[:, rows:], axis=0)], axis=0
    )
    moved = gather_x(moved)
    middle = gather(jnp.sum(moved[:, -slab:], axis=0), ("y", "core")).reshape(width, width)
    row_product = moved[:, :-slab].reshape(4, -1, rows, width).transpose(1, 0, 2, 3).reshape(-1, width)

    upper, inverse = factor(gram_matrix)
    row_basis = dot(row_panel, inverse, ((1,), (1,)))
    col_basis = dot(col_panel, inverse, ((1,), (1,)))

    coupling = dot(inverse, dot(middle, inverse, ((1,), (1,))))
    left = jnp.concatenate([row_basis, row_product], axis=1)
    right = jnp.concatenate(
        [
            2.0 * dot(col_product, inverse, ((1,), (1,))) - 2.0 * dot(col_basis, coupling + coupling.T),
            2.0 * dot(col_basis, inverse),
        ],
        axis=1,
    )
    updated = trailing - dot(left, right, ((1,), (1,)), CLOSE)
    rotated = vectors - 2.0 * dot(row_basis, dot(inverse, projected, ((1,), (1,))))
    return (upper, updated, rotated)


def solution(mesh):
    fine = Mesh(mesh.devices.reshape(4, 2, 8, 4), ("y", "core", "z", "x"))
    row, col = ("y", "core"), ("z", "x")
    return jax.shard_map(
        shards,
        mesh=fine,
        in_specs=(P(row + col, None), P(row, col), P(row, col)),
        out_specs=(P(), P(row, col), P(row, col)),
        check_vma=False,
    )
```

```python
import functools
import jax
import jax.numpy as jnp
from jax import lax
from jax.experimental import pallas as pl
from jax.experimental.pallas import tpu as pltpu
from jax.sharding import Mesh, PartitionSpec as P

EVERYWHERE = ("y", "core", "z", "x")
PARTS = 4


def dot(left, right, dims=((1,), (0,))):
    return lax.dot_general(
        left,
        right,
        (dims, ((), ())),
        precision=lax.Precision.HIGHEST,
        preferred_element_type=jnp.float32,
    )


def shift(x, axis, step):
    n = lax.axis_size(axis)
    return lax.ppermute(x, axis, [(i, (i + step) % n) for i in range(n)])


def swap_core(x):
    return lax.ppermute(x, "core", [(0, 1), (1, 0)])


def device(y, core, z, x):
    return ((y * 2 + core) * 8 + z) * 4 + x


def gather_z(x):
    half = x.shape[0] // 2
    low2, high2 = shift(x, "z", 2), shift(x, "z", -2)
    low1, high1 = shift(x, "z", 1), shift(x, "z", -1)
    low3, high3 = shift(low2, "z", 1), shift(high2, "z", -1)
    far = [shift(low2[:half], "z", 2), shift(high2[half:], "z", -2)]
    return [x, high1, high2, high3, jnp.concatenate(far, axis=0), low3, low2, low1]


def gather_x(first, second):
    low_a, high_b = shift(first, "x", 1), shift(second, "x", -1)
    low_b, high_a = shift(second, "x", 1), shift(first, "x", -1)
    far = (shift(low_a, "x", 1), shift(high_b, "x", -1))
    return [(first, second), (high_a, high_b), far, (low_a, low_b)]


def gather_row(x):
    own = jnp.stack([x] + [shift(x, "y", step) for step in (1, 2, 3)])
    return own, swap_core(own)


def pick(ids, own, other, at):
    y, core = at // 2, at % 2
    place = lax.rem(ids[0] - y + 4, 4)
    return jnp.where(ids[1] == core, own[place], other[place])


def whole(ids, own, other):
    return jnp.concatenate([pick(ids, own, other, at) for at in range(8)], axis=0)


def call(kernel, ids, operands, in_specs, out_shape, out_specs, flops, aliases=None, scratch=()):
    spec = pltpu.PrefetchScalarGridSpec(
        num_scalar_prefetch=1,
        grid=(1,),
        in_specs=in_specs,
        out_specs=out_specs,
        scratch_shapes=scratch,
    )
    size = sum(o.size * 4 for o in operands[:2])
    return pl.pallas_call(
        kernel,
        grid_spec=spec,
        out_shape=out_shape,
        input_output_aliases=aliases or {},
        cost_estimate=pl.CostEstimate(flops=int(flops), bytes_accessed=size, transcendentals=0),
        compiler_params=pltpu.CompilerParams(vmem_limit_bytes=40 * 1024 * 1024),
    )(ids, *operands)


def full(shape):
    return pl.BlockSpec(shape, lambda i, ids: (0,) * len(shape))


def f32(*shape):
    return jax.ShapeDtypeStruct(shape, jnp.float32)


def absorb_kernel(start, ids, trailing, first, second, *rest):
    if start:
        product, gram, rows = rest
    else:
        product_in, gram_in, _, product, gram, rows = rest
    n, width = first.shape[1:]
    panel = jnp.concatenate([first[...].reshape(-1, width), second[...].reshape(-1, width)], axis=0)
    places = [lax.rem(ids[2] + step, 8) for step in range(8)]
    for step, place in enumerate(places):
        rows[place, 0] = panel[step * n : (step + 1) * n]
    block = jnp.concatenate([trailing[place, 0] for place in places], axis=0)
    flat = panel.T
    more_product, more_gram = dot(flat, block), dot(flat, panel)
    if start:
        product[...], gram[...] = more_product, more_gram
    else:
        product[...], gram[...] = product_in[...] + more_product, gram_in[...] + more_gram


def absorb(ids, offset, trailing, piece, state):
    n, width = piece[0].shape[1:]
    span = trailing.shape[-1]
    at = lambda i, ids: (0, lax.rem(ids[3] + offset, 4), 0, 0)
    half = full((4, n, width))
    in_specs = [pl.BlockSpec((8, 1, n, span), at), half, half]
    sums = [full((width, span)), full((width, width))]
    operands = [trailing, *piece]
    aliases = {}
    if state is not None:
        in_specs += sums + [pl.BlockSpec(memory_space=pl.ANY)]
        operands += state
        aliases = {4: 0, 5: 1, 6: 2}
    return call(
        functools.partial(absorb_kernel, state is None),
        ids,
        operands,
        in_specs,
        [f32(width, span), f32(width, width), f32(8, 4, n, width)],
        sums + [pl.BlockSpec((8, 1, n, width), at)],
        12 * 8 * n * width * (span + width),
        aliases,
    )


def pack_kernel(ids, product, gram, own, other, keep, send):
    width = gram.shape[0]
    n, slab = product.shape[1] // 8, width // 8
    panel = whole(ids, own, other)
    middle = dot(product[...], panel)
    tall = product[...].T
    sums = gram[...]
    for y in range(4):
        both = []
        for at in (2 * y, 2 * y + 1):
            both.append(
                jnp.concatenate(
                    [
                        tall[at * n : (at + 1) * n],
                        middle[at * slab : (at + 1) * slab],
                        sums[at * slab : (at + 1) * slab],
                    ],
                    axis=0,
                )
            )
        keep[y] = jnp.where(ids[1] == 0, both[0], both[1])
        send[y] = jnp.where(ids[1] == 0, both[1], both[0])


def pack(ids, product, gram, columns):
    width, span = product.shape
    rows = (span + 2 * width) // 8
    block = full((4, span // 8, width))
    return call(
        pack_kernel,
        ids,
        [product, gram, *columns],
        [full((width, span)), full((width, width)), block, block],
        [f32(4, rows, width)] * 2,
        [full((4, rows, width))] * 2,
        12 * span * width * width,
    )


def route_kernel(ids, keep, got, *outs):
    for step, out in enumerate(outs):
        place = lax.rem(ids[0] + step, 4)
        out[...] = keep[place] + got[place]


def route(ids, keep, got):
    shape = keep.shape[1:]
    return call(
        route_kernel,
        ids,
        [keep, got],
        [full(keep.shape)] * 2,
        [f32(*shape)] * 4,
        [full(shape)] * 4,
        keep.size,
    )


def factor_kernel(part, ids, *refs):
    if part == 0:
        own, other, work = refs
        work[...] = whole(ids, own, other)
    elif part < PARTS - 1:
        work = refs[1]
        work[...] = refs[0][...]
    else:
        upper, inverse, work = refs[1:]
        work[...] = refs[0][...]
    n = work.shape[0]
    half, size = n // 2, n // PARTS
    lane = lax.broadcasted_iota(jnp.int32, (8, half), 1)
    sub = lax.broadcasted_iota(jnp.int32, (8, half), 0)
    base, rest = part * size, (part + 1) * size
    tiles = [
        [work[base + t : base + t + 8, h * half : (h + 1) * half] for h in (0, 1)]
        for t in range(0, size, 8)
    ]
    for j in range(size):
        side, at = (base + j) // half, (base + j) % half
        own, s = j // 8, j % 8
        scale = lax.rsqrt(tiles[own][side][s : s + 1, at : at + 1])
        pivot = [tiles[own][h][s : s + 1, :] * scale for h in (0, 1)]
        pivot[side] = jnp.where(lane[:1] == at, scale, pivot[side])
        for t in range(own, size // 8):
            weight = tiles[t][side][:, at : at + 1] * scale
            for h in (0, 1):
                old = tiles[t][h]
                kept = jnp.where(lane == at, 0.0, old) if h == side else old
                new = kept - weight * pivot[h]
                if t == own:
                    new = jnp.where(sub > s, new, jnp.where(sub == s, pivot[h], old))
                tiles[t][h] = new
    rows = jnp.concatenate([jnp.concatenate(t, axis=1) for t in tiles], axis=0)
    work[base:rest, :] = rows
    if part < PARTS - 1:
        wide = lax.broadcasted_iota(jnp.int32, (size, n), 1)
        tall = lax.broadcasted_iota(jnp.int32, (size, n), 0) + base
        lower_rows = jnp.where((wide > tall) & (wide < rest), 0.0, rows)
        change = dot(rows, lower_rows, ((0,), (0,)))
        wide = lax.broadcasted_iota(jnp.int32, (n - rest, n), 1)
        below = jnp.where((wide >= base) & (wide < rest), 0.0, work[rest:, :])
        work[rest:, :] = below - change[rest:, :]
    else:
        done = work[...]
        wide = lax.broadcasted_iota(jnp.int32, (n, n), 1)
        tall = lax.broadcasted_iota(jnp.int32, (n, n), 0)
        upper[...] = jnp.where(wide > tall, done, jnp.where(wide == tall, 1.0 / done, 0.0))
        inverse[...] = jnp.where(wide <= tall, done, 0.0)


def factor(ids, own, other):
    n = own.shape[-1]
    square = full((n, n))
    state = None
    for part in range(PARTS):
        last = part == PARTS - 1
        state = call(
            functools.partial(factor_kernel, part),
            ids,
            [own, other] if part == 0 else [state],
            [full(own.shape)] * 2 if part == 0 else [square],
            [f32(n, n)] * 2 if last else f32(n, n),
            [square] * 2 if last else square,
            5e9,
            None,
            [pltpu.VMEM((n, n), jnp.float32)] if last else (),
        )
    return state


def prepare_kernel(ids, inverse, p_own, p_other, w_own, w_other, t_own, t_other, right):
    solve = inverse[...]
    width = solve.shape[0]
    panel = dot(solve, whole(ids, p_own, p_other), ((1,), (1,)))
    product = dot(solve, whole(ids, w_own, w_other), ((1,), (1,)))
    middle = dot(whole(ids, t_own, t_other), solve, ((1,), (1,)))
    coupling = dot(solve, middle)
    zeta = 2.0 * product - 2.0 * dot(coupling + coupling.T, panel)
    back = solve.T
    right[:width] = dot(back, zeta)
    right[width:] = 2.0 * dot(back, panel)


def prepare(ids, inverse, columns, products, middles):
    width = inverse.shape[0]
    span = 8 * columns[0].shape[1]
    operands = [inverse, *columns, *products, *middles]
    return call(
        prepare_kernel,
        ids,
        operands,
        [full(o.shape) for o in operands],
        f32(2 * width, span),
        full((2 * width, span)),
        12 * width * width * (5 * span + 2 * width),
    )


def update_kernel(start, ids, trailing, rows, first, second, right, *rest):
    out, left = rest[-2:]
    n, width = first.shape[1:]
    left[:, :, :width] = rows[...].reshape(8, n, width)
    for step in range(8):
        piece = first[step] if step < 4 else second[step - 4]
        left[lax.rem(ids[2] + step, 8), :, width:] = piece
    out[...] = trailing[...] - dot(left[...].reshape(8 * n, 2 * width), right[...])


def update(ids, offset, trailing, rows, piece, right, out):
    n, width = piece[0].shape[1:]
    span = trailing.shape[1]
    at = lambda i, ids: (lax.rem(ids[3] + offset, 4), 0)
    half = full((4, n, width))
    block = pl.BlockSpec((8 * n, span), at)
    in_specs = [block, pl.BlockSpec((8 * n, width), at), half, half, full(right.shape)]
    operands = [trailing, rows, *piece, right]
    aliases = {}
    if out is not None:
        in_specs.append(pl.BlockSpec(memory_space=pl.ANY))
        operands.append(out)
        aliases = {6: 0}
    return call(
        functools.partial(update_kernel, out is None),
        ids,
        operands,
        in_specs,
        f32(*trailing.shape),
        block,
        12 * 8 * n * 2 * width * span,
        aliases,
        [pltpu.VMEM((8, n, 2 * width), jnp.float32)],
    )


def shards(panel, trailing, vectors):
    n, width = panel.shape
    slab = width // 8
    ids = jnp.stack([lax.axis_index(a) for a in EVERYWHERE]).astype(jnp.int32)
    by_cols = [(c * 8 + r, r * 32 + c) for r in range(8) for c in range(32)]
    turn = [
        (device(y, core, z, x), device(z // 2, z % 2, 2 * y + core, x))
        for y in range(4)
        for core in range(2)
        for z in range(8)
        for x in range(4)
    ]

    columns = gather_row(lax.ppermute(panel, EVERYWHERE, by_cols))
    blocks = gather_z(panel)
    pieces = gather_x(jnp.stack(blocks[:4]), jnp.stack(blocks[4:]))
    cut = trailing.reshape(8, 4, n, -1)
    state = None
    for offset in (0, 3, 1, 2):
        state = absorb(ids, offset, cut, pieces[offset], state)
    product, gram, rows = state
    rows = rows.reshape(-1, width)

    projected = dot(vectors, rows, ((0,), (0,)))
    projected = projected + swap_core(projected)
    projected = projected + sum(shift(projected, "y", step) for step in (1, 2, 3))

    keep, send = pack(ids, product, gram, columns)
    routed = route(ids, keep, swap_core(send))
    total = routed[0]
    for step in (1, 2, 3):
        total = total + shift(routed[step], "y", step)
    own_product, own_middle, own_gram = total[:n], total[n : n + slab], total[n + slab :]

    grams = gather_row(own_gram)
    products = gather_row(own_product)
    own_middle = own_middle + sum(shift(own_middle, "x", step) for step in (1, 2, 3))
    turned = lax.ppermute(own_product, EVERYWHERE, turn)
    blocks = gather_z(jnp.concatenate([turned, own_middle], axis=0))
    middles = gather_row(sum(b[n:] for b in blocks))
    blocks = [b[:n] for b in blocks]
    pieces = gather_x(jnp.stack(blocks[:4]), jnp.stack(blocks[4:]))

    upper, inverse = factor(ids, *grams)
    right = prepare(ids, inverse, columns, products, middles)
    updated = None
    for offset in (0, 3, 1, 2):
        updated = update(ids, offset, trailing, rows, pieces[offset], right, updated)
    turns = 2.0 * dot(dot(projected, inverse, ((1,), (1,))), inverse)
    rotated = vectors - dot(rows, turns, ((1,), (1,)))
    return (upper, updated, rotated)


def solution(mesh):
    fine = Mesh(mesh.devices.reshape(4, 2, 8, 4), EVERYWHERE)
    row, col = ("y", "core"), ("z", "x")
    return jax.shard_map(
        shards,
        mesh=fine,
        in_specs=(P(row + col, None), P(row, col), P(row, col)),
        out_specs=(P(), P(row, col), P(row, col)),
        check_vma=False,
    )
```

```python
import functools
import jax
import jax.numpy as jnp
from jax import lax
from jax.experimental import pallas as pl
from jax.experimental.pallas import tpu as pltpu
from jax.sharding import Mesh, PartitionSpec as P

EVERYWHERE = ("y", "core", "z", "x")
BLOCK = 64


def dot(left, right, dims=((1,), (0,))):
    return lax.dot_general(
        left,
        right,
        (dims, ((), ())),
        precision=lax.Precision.HIGHEST,
        preferred_element_type=jnp.float32,
    )


def shift(x, axis, step):
    n = lax.axis_size(axis)
    return lax.ppermute(x, axis, [(i, (i + step) % n) for i in range(n)])


def swap_core(x):
    return lax.ppermute(x, "core", [(0, 1), (1, 0)])


def device(y, core, z, x):
    return ((y * 2 + core) * 8 + z) * 4 + x


def gather_z(x):
    half = x.shape[0] // 2
    low2, high2 = shift(x, "z", 2), shift(x, "z", -2)
    low1, high1 = shift(x, "z", 1), shift(x, "z", -1)
    low3, high3 = shift(low2, "z", 1), shift(high2, "z", -1)
    far = [shift(low2[:half], "z", 2), shift(high2[half:], "z", -2)]
    return [x, high1, high2, high3, *far, low3, low2, low1]


def gather_x(first, second):
    low_a, high_b = shift(first, "x", 1), shift(second, "x", -1)
    low_b, high_a = shift(second, "x", 1), shift(first, "x", -1)
    far = (shift(low_a, "x", 1), shift(high_b, "x", -1))
    return [(first, second), (high_a, high_b), far, (low_a, low_b)]


def gather_row(x):
    own = jnp.stack([x] + [shift(x, "y", step) for step in (1, 2, 3)])
    return own, swap_core(own)


def pick(ids, own, other, at, start, stop):
    y, core = at // 2, at % 2
    place = lax.rem(ids[0] - y + 4, 4)
    return jnp.where(ids[1] == core, own[place, start:stop], other[place, start:stop])


def whole(ids, own, other, start, stop):
    return jnp.concatenate([pick(ids, own, other, at, start, stop) for at in range(8)], axis=0)


def call(kernel, ids, operands, in_specs, out_shape, out_specs, flops, aliases=None, scratch=()):
    spec = pltpu.PrefetchScalarGridSpec(
        num_scalar_prefetch=1,
        grid=(1,),
        in_specs=in_specs,
        out_specs=out_specs,
        scratch_shapes=scratch,
    )
    size = sum(o.size * 4 for o in operands[:2])
    return pl.pallas_call(
        kernel,
        grid_spec=spec,
        out_shape=out_shape,
        input_output_aliases=aliases or {},
        cost_estimate=pl.CostEstimate(flops=int(flops), bytes_accessed=size, transcendentals=0),
        compiler_params=pltpu.CompilerParams(vmem_limit_bytes=40 * 1024 * 1024),
    )(ids, *operands)


def full(shape):
    return pl.BlockSpec(shape, lambda i, ids: (0,) * len(shape))


def f32(*shape):
    return jax.ShapeDtypeStruct(shape, jnp.float32)


def absorb_kernel(start, ids, trailing, first, second, *rest):
    if start:
        product, gram, rows = rest
    else:
        product_in, gram_in, _, product, gram, rows = rest
    n, width = first.shape[1:]
    panel = jnp.concatenate([first[...].reshape(-1, width), second[...].reshape(-1, width)], axis=0)
    places = [lax.rem(ids[2] + step, 8) for step in range(8)]
    for step, place in enumerate(places):
        rows[place, 0] = panel[step * n : (step + 1) * n]
    block = jnp.concatenate([trailing[place, 0] for place in places], axis=0)
    flat = panel.T
    more_product, more_gram = dot(flat, block), dot(flat, panel)
    if start:
        product[...], gram[...] = more_product, more_gram
    else:
        product[...], gram[...] = product_in[...] + more_product, gram_in[...] + more_gram


def absorb(ids, offset, trailing, piece, state):
    n, width = piece[0].shape[1:]
    span = trailing.shape[-1]
    at = lambda i, ids: (0, lax.rem(ids[3] + offset, 4), 0, 0)
    half = full((4, n, width))
    in_specs = [pl.BlockSpec((8, 1, n, span), at), half, half]
    sums = [full((width, span)), full((width, width))]
    operands = [trailing, *piece]
    aliases = {}
    if state is not None:
        in_specs += sums + [pl.BlockSpec(memory_space=pl.ANY)]
        operands += state
        aliases = {4: 0, 5: 1, 6: 2}
    return call(
        functools.partial(absorb_kernel, state is None),
        ids,
        operands,
        in_specs,
        [f32(width, span), f32(width, width), f32(8, 4, n, width)],
        sums + [pl.BlockSpec((8, 1, n, width), at)],
        12 * 8 * n * width * (span + width),
        aliases,
    )


def arrange_kernel(ids, *refs):
    blocks, panel, (first, second, copy) = refs[:9], refs[9], refs[10:]
    half = blocks[4].shape[0]
    for step in range(4):
        first[step] = blocks[step][...]
    second[0, :half] = blocks[4][...]
    second[0, half:] = blocks[5][...]
    for step in range(1, 4):
        second[step] = blocks[step + 5][...]
    copy[...] = panel[...]


def arrange(ids, blocks, panel):
    n, width = panel.shape
    operands = [*blocks, panel]
    shapes = [(4, n, width), (4, n, width), (n, width)]
    return call(
        arrange_kernel,
        ids,
        operands,
        [full(o.shape) for o in operands],
        [f32(*s) for s in shapes],
        [full(s) for s in shapes],
        1e6,
    )


def pack_kernel(ids, product, gram, own, other, vectors, rows, keep, send):
    width = gram.shape[0]
    n, slab, eig = product.shape[1] // 8, width // 8, vectors.shape[0]
    panel = whole(ids, own, other, 0, n)
    middle = dot(product[...], panel)
    tall = product[...].T
    sums = gram[...]
    line = lax.broadcasted_iota(jnp.int32, (64, eig), 0)
    spot = lax.broadcasted_iota(jnp.int32, (64, eig), 1)
    per = eig // 8
    pad = jnp.where((line % 8 < per) & (spot == line // 8 * per + line % 8), 1.0, 0.0)
    projected = dot(pad, dot(vectors[...], rows[...]))
    for y in range(4):
        both = []
        for at in (2 * y, 2 * y + 1):
            both.append(
                jnp.concatenate(
                    [
                        tall[at * n : (at + 1) * n],
                        sums[at * slab : (at + 1) * slab],
                        projected[at * 8 : (at + 1) * 8],
                        middle[at * slab : (at + 1) * slab],
                    ],
                    axis=0,
                )
            )
        keep[y] = jnp.where(ids[1] == 0, both[0], both[1])
        send[y] = jnp.where(ids[1] == 0, both[1], both[0])


def pack(ids, product, gram, columns, vectors, rows):
    width, span = product.shape
    depth = (span + 2 * width) // 8 + 8
    operands = [product, gram, *columns, vectors, rows]
    return call(
        pack_kernel,
        ids,
        operands,
        [full(o.shape) for o in operands],
        [f32(4, depth, width)] * 2,
        [full((4, depth, width))] * 2,
        12 * span * width * width,
    )


def route_kernel(ids, keep, got, *outs):
    for step, out in enumerate(outs):
        place = lax.rem(ids[0] + step, 4)
        out[...] = keep[place] + got[place]


def route(ids, keep, got):
    shape = keep.shape[1:]
    return call(
        route_kernel,
        ids,
        [keep, got],
        [full(keep.shape)] * 2,
        [f32(*shape)] * 4,
        [full(shape)] * 4,
        keep.size,
    )


def settle_kernel(ids, *refs):
    parts, (shared, product, middle) = refs[:4], refs[4:]
    total = parts[0][...] + parts[1][...] + parts[2][...] + parts[3][...]
    shared[...] = total[: shared.shape[0]]
    product[...] = total[: product.shape[0]]
    middle[...] = total[shared.shape[0] :]


def settle(ids, parts, n, slab):
    depth, width = parts[0].shape
    shapes = [(depth - slab, width), (n, width), (slab, width)]
    return call(
        settle_kernel,
        ids,
        parts,
        [full((depth, width))] * 4,
        [f32(*s) for s in shapes],
        [full(s) for s in shapes],
        1e6,
    )


def spread_kernel(ids, product, *refs):
    parts, out = refs[:-1], refs[-1]
    n = product.shape[0]
    middle = parts[0][...] + parts[1][...] + parts[2][...] + parts[3][...]
    for step in range(8):
        out[step, :n] = product[...]
        out[step, n:] = middle


def spread(ids, product, parts):
    n, width = product.shape
    slab = parts[0].shape[0]
    operands = [product, *parts]
    return call(
        spread_kernel,
        ids,
        operands,
        [full(o.shape) for o in operands],
        f32(8, n + slab, width),
        full((8, n + slab, width)),
        1e6,
    )


def split_kernel(ids, blocks, first, second, middle):
    n = first.shape[1]
    total = blocks[0, n:]
    for step in range(1, 8):
        total = total + blocks[step, n:]
    first[...] = blocks[:4, :n]
    second[...] = blocks[4:, :n]
    middle[...] = total


def split(ids, blocks, n):
    _, depth, width = blocks.shape
    shapes = [(4, n, width), (4, n, width), (depth - n, width)]
    return call(
        split_kernel,
        ids,
        [blocks],
        [full(blocks.shape)],
        [f32(*s) for s in shapes],
        [full(s) for s in shapes],
        1e6,
    )


def eliminate(values, scales, factors):
    done = []
    for i, value in enumerate(values):
        for k in range(i):
            value = value - factors[k][i] * done[k]
        done.append(value * scales[i])
    return done

def factor_kernel(start, ids, gram_own, gram_other, upper, inverse, work):
    n = work.shape[0]
    half, block = n // 2, BLOCK
    work[...] = whole(ids, gram_own, gram_other, start, start + n // 8)
    lane = lax.broadcasted_iota(jnp.int32, (8, half), 1)
    sub = lax.broadcasted_iota(jnp.int32, (8, half), 0)
    spread = lambda v: jnp.broadcast_to(v, (8, half))
    for base in range(0, n, block):
        rest = base + block
        tiles = [[work[base + t : base + t + 8, h * half : (h + 1) * half] for h in (0, 1)] for t in range(0, block, 8)]
        for own in range(block // 8):
            side, at = (base + 8 * own) // half, (base + 8 * own) % half
            tile = tiles[own]
            cols = [spread(tile[side][:, at + k : at + k + 1]) for k in range(8)]
            scales, factors = [], []
            for i in range(8):
                d = spread(cols[i][i : i + 1])
                for k in range(i):
                    d = d - factors[k][i] * factors[k][i]
                scales.append(lax.rsqrt(d))
                line = [None] * 8
                for m in range(i + 1, 8):
                    u = spread(cols[m][i : i + 1])
                    for k in range(i):
                        u = u - factors[k][i] * factors[k][m]
                    line[m] = u * scales[i]
                factors.append(line)
            lines = [[spread(tile[h][k : k + 1]) for k in range(8)] for h in (0, 1)]
            inside = (lane >= at) & (lane < at + 8)
            full = eliminate(lines[side], scales, factors)
            lines[side] = [jnp.where(lane == at + k, 1.0, jnp.where(inside, 0.0, v)) for k, v in enumerate(lines[side])]
            lines = [eliminate(lines[h], scales, factors) for h in (0, 1)]
            for t in range(own + 1, block // 8):
                weights = eliminate([spread(tiles[t][side][:, at + k : at + k + 1]) for k in range(8)], scales, factors)
                for h in (0, 1):
                    value = tiles[t][h]
                    if h == side:
                        value = jnp.where(inside, 0.0, value)
                    for k in range(8):
                        value = value - weights[k] * lines[h][k]
                    tiles[t][h] = value
            for h in (0, 1):
                value = lines[h][0]
                for k in range(1, 8):
                    value = jnp.where(sub == k, lines[h][k], value)
                if h == side:
                    above = full[0]
                    for k in range(1, 8):
                        above = jnp.where(sub == k, full[k], above)
                    value = jnp.where(inside & (lane > at + sub), above, value)
                tile[h] = value
        rows = jnp.concatenate([jnp.concatenate(t, axis=1) for t in tiles], axis=0)
        work[base:rest, :] = rows
        if rest < n:
            wide = lax.broadcasted_iota(jnp.int32, (block, n), 1)
            tall = lax.broadcasted_iota(jnp.int32, (block, n), 0) + base
            lower_rows = jnp.where((wide > tall) & (wide < rest), 0.0, rows)
            change = dot(rows, lower_rows, ((0,), (0,)))
            wide = lax.broadcasted_iota(jnp.int32, (n - rest, n), 1)
            below = jnp.where((wide >= base) & (wide < rest), 0.0, work[rest:, :])
            work[rest:, :] = below - change[rest:, :]
    done = work[...]
    wide = lax.broadcasted_iota(jnp.int32, (n, n), 1)
    tall = lax.broadcasted_iota(jnp.int32, (n, n), 0)
    upper[...] = jnp.where(wide > tall, done, jnp.where(wide == tall, 1.0 / done, 0.0))
    inverse[...] = jnp.where(wide <= tall, done, 0.0)

def factor(ids, shared, start):
    n = shared[0].shape[-1]
    return call(
        functools.partial(factor_kernel, start),
        ids,
        shared,
        [full(shared[0].shape)] * 2,
        [f32(n, n)] * 2,
        [full((n, n))] * 2,
        1e10,
        None,
        [pltpu.VMEM((n, n), jnp.float32)],
    )


def prepare_kernel(ids, inverse, p_own, p_other, s_own, s_other, t_own, t_other, right, turns):
    solve = inverse[...]
    width = solve.shape[0]
    n, slab = p_own.shape[1], width // 8
    panel = dot(solve, whole(ids, p_own, p_other, 0, n), ((1,), (1,)))
    product = dot(solve, whole(ids, s_own, s_other, 0, n), ((1,), (1,)))
    middle = dot(whole(ids, t_own, t_other, 0, slab), solve, ((1,), (1,)))
    coupling = dot(solve, middle)
    zeta = 2.0 * product - 2.0 * dot(coupling + coupling.T, panel)
    back = solve.T
    right[:width] = dot(back, zeta)
    right[width:] = 2.0 * dot(back, panel)
    projected = whole(ids, s_own, s_other, n + slab, n + slab + 8)
    turns[...] = 2.0 * dot(dot(projected, back), solve)


def prepare(ids, inverse, columns, shared, middles):
    width = inverse.shape[0]
    span = 8 * columns[0].shape[1]
    operands = [inverse, *columns, *shared, *middles]
    shapes = [(2 * width, span), (64, width)]
    return call(
        prepare_kernel,
        ids,
        operands,
        [full(o.shape) for o in operands],
        [f32(*s) for s in shapes],
        [full(s) for s in shapes],
        12 * width * width * (5 * span + 2 * width),
    )


def update_kernel(start, ids, trailing, rows, first, second, right, *rest):
    out, left = rest[-2:]
    n, width = first.shape[1:]
    left[:, :, :width] = rows[...].reshape(8, n, width)
    for step in range(8):
        piece = first[step] if step < 4 else second[step - 4]
        left[step, :, width:] = piece
    out[...] = trailing[...] - dot(left[...].reshape(8 * n, 2 * width), right[...])


def update(ids, offset, trailing, rows, piece, right, out):
    n, width = piece[0].shape[1:]
    span = trailing.shape[1]
    at = lambda i, ids: (lax.rem(ids[3] + offset, 4), 0)
    half = full((4, n, width))
    block = pl.BlockSpec((8 * n, span), at)
    in_specs = [block, pl.BlockSpec((8 * n, width), at), half, half, full(right.shape)]
    operands = [trailing, rows, *piece, right]
    aliases = {}
    if out is not None:
        in_specs.append(pl.BlockSpec(memory_space=pl.ANY))
        operands.append(out)
        aliases = {6: 0}
    return call(
        functools.partial(update_kernel, out is None),
        ids,
        operands,
        in_specs,
        f32(*trailing.shape),
        block,
        12 * 8 * n * 2 * width * span,
        aliases,
        [pltpu.VMEM((8, n, 2 * width), jnp.float32)],
    )


def shards(panel, trailing, vectors):
    n, width = panel.shape
    slab = width // 8
    ids = jnp.stack([lax.axis_index(a) for a in EVERYWHERE]).astype(jnp.int32)
    by_cols = [(c * 8 + r, r * 32 + c) for r in range(8) for c in range(32)]
    turn = [
        (device(y, core, z, x), device(z // 2, z % 2, 2 * y + core, x))
        for y in range(4)
        for core in range(2)
        for z in range(8)
        for x in range(4)
    ]

    first, second, copy = arrange(ids, gather_z(panel), panel)
    pieces = gather_x(first, second)
    columns = gather_row(lax.ppermute(copy, EVERYWHERE, by_cols))
    cut = trailing.reshape(8, 4, n, -1)
    state = None
    for offset in (0, 3, 1, 2):
        state = absorb(ids, offset, cut, pieces[offset], state)
    product, gram, rows = state
    rows = rows.reshape(-1, width)

    keep, send = pack(ids, product, gram, columns, vectors.T, rows)
    routed = route(ids, keep, swap_core(send))
    parts = [routed[0]] + [shift(routed[step], "y", step) for step in (1, 2, 3)]
    share, own_product, own_middle = settle(ids, parts, n, slab)

    shared = gather_row(share)
    turned = lax.ppermute(own_product, EVERYWHERE, turn)
    parts = [own_middle] + [shift(own_middle, "x", step) for step in (1, 2, 3)]
    blocks = lax.all_to_all(spread(ids, turned, parts), "z", 0, 0)
    upper, inverse = factor(ids, shared, n)
    first, second, middle = split(ids, blocks, n)
    pieces = gather_x(first, second)
    middles = gather_row(middle)

    right, turns = prepare(ids, inverse, columns, shared, middles)
    updated = None
    for offset in (0, 3, 1, 2):
        updated = update(ids, offset, trailing, rows, pieces[offset], right, updated)
    turns = turns.reshape(8, 8, width)[:, : vectors.shape[1] // 8].reshape(-1, width)
    rotated = vectors - dot(rows, turns, ((1,), (1,)))
    return (upper, updated, rotated)


def solution(mesh):
    fine = Mesh(mesh.devices.reshape(4, 2, 8, 4), EVERYWHERE)
    row, col = ("y", "core"), ("z", "x")
    return jax.shard_map(
        shards,
        mesh=fine,
        in_specs=(P(row + col, None), P(row, col), P(row, col)),
        out_specs=(P(), P(row, col), P(row, col)),
        check_vma=False,
    )
```

```python
import functools
import jax
import jax.numpy as jnp
from jax import lax
from jax.experimental import pallas as pl
from jax.experimental.pallas import tpu as pltpu
from jax.sharding import Mesh, PartitionSpec as P

EVERYWHERE = ("y", "core", "z", "x")
BLOCK = 64
COST = 0.001
GRANT = 9 * 1024 * 1024
WIDE_GRANT = 48 * 1024 * 1024


def dot(left, right, dims=((1,), (0,))):
    return lax.dot_general(
        left,
        right,
        (dims, ((), ())),
        precision=lax.Precision.HIGHEST,
        preferred_element_type=jnp.float32,
    )


def shift(x, axis, step):
    n = lax.axis_size(axis)
    return lax.ppermute(x, axis, [(i, (i + step) % n) for i in range(n)])


def swap_core(x):
    return lax.ppermute(x, "core", [(0, 1), (1, 0)])


def device(y, core, z, x):
    return ((y * 2 + core) * 8 + z) * 4 + x


def gather_z(x):
    half = x.shape[0] // 2
    low2, high2 = shift(x, "z", 2), shift(x, "z", -2)
    low1, high1 = shift(x, "z", 1), shift(x, "z", -1)
    low3, high3 = shift(low2, "z", 1), shift(high2, "z", -1)
    far = [shift(low2[:half], "z", 2), shift(high2[half:], "z", -2)]
    return [x, high1, high2, high3, *far, low3, low2, low1]


def gather_x(first, second):
    low_a, high_b = shift(first, "x", 1), shift(second, "x", -1)
    low_b, high_a = shift(second, "x", 1), shift(first, "x", -1)
    far = (shift(low_a, "x", 1), shift(high_b, "x", -1))
    return [(first, second), (high_a, high_b), far, (low_a, low_b)]


def all_to_row(copies):
    return lax.all_to_all(copies, ("y", "core"), 0, 0)


def gather_row(x):
    own = jnp.stack([x] + [shift(x, "y", step) for step in (1, 2, 3)])
    return own, swap_core(own)


def pick(ids, own, other, start, stop):
    blocks = []
    for y in range(4):
        place = lax.rem(ids[0] - y + 4, 4)
        for core in (0, 1):
            blocks.append(jnp.where(ids[1] == core, own[place, start:stop], other[place, start:stop]))
    return jnp.concatenate(blocks, axis=0)


def whole(blocks, start, stop):
    return blocks[:, start:stop].reshape(-1, blocks.shape[-1])


def call(
    kernel, ids, operands, in_specs, out_shape, out_specs, flops, aliases=None, scratch=(), steps=1, grant=GRANT
):
    spec = pltpu.PrefetchScalarGridSpec(
        num_scalar_prefetch=1,
        grid=(steps,),
        in_specs=in_specs,
        out_specs=out_specs,
        scratch_shapes=scratch,
    )
    size = sum(o.size * 4 for o in operands[:2])
    return pl.pallas_call(
        kernel,
        grid_spec=spec,
        out_shape=out_shape,
        input_output_aliases=aliases or {},
        cost_estimate=pl.CostEstimate(flops=int(flops * COST), bytes_accessed=int(size * COST), transcendentals=0),
        compiler_params=pltpu.CompilerParams(vmem_limit_bytes=grant),
    )(ids, *operands)


def full(shape):
    return pl.BlockSpec(shape, lambda i, ids: (0,) * len(shape))


def f32(*shape):
    return jax.ShapeDtypeStruct(shape, jnp.float32)


def add_piece(trailing, piece):
    flat = piece.T
    return dot(flat, trailing.reshape(piece.shape[0], -1)), dot(flat, piece)


def in_place(ids, piece):
    return jnp.stack([piece[lax.rem(z - ids[2] + 8, 8)] for z in range(8)])


def absorb_kernel(ids, trailing, *refs):
    pieces, (product, gram, rows, piece) = refs[:6], refs[6:]
    step = pl.program_id(0)
    for at in range(3):

        @pl.when(step == at)
        def _():
            piece[:4] = pieces[2 * at][...]
            piece[4:] = pieces[2 * at + 1][...]

    panel = in_place(ids, piece)
    rows[:, 0] = panel
    more_product, more_gram = add_piece(trailing[:, 0], panel.reshape(-1, panel.shape[-1]))

    @pl.when(step == 0)
    def _():
        product[...], gram[...] = more_product, more_gram

    @pl.when(step > 0)
    def _():
        product[...], gram[...] = product[...] + more_product, gram[...] + more_gram


def absorb(ids, trailing, pieces):
    n, width = pieces[0][0].shape[1:]
    span = trailing.shape[-1]
    at = lambda i, ids: (0, lax.rem(ids[3] + lax.rem(3 * i, 5), 4), 0, 0)
    parts = [half for piece in pieces for half in piece]
    return call(
        absorb_kernel,
        ids,
        [trailing, *parts],
        [pl.BlockSpec((8, 1, n, span), at)] + [full(o.shape) for o in parts],
        [f32(width, span), f32(width, width), f32(8, 4, n, width)],
        [full((width, span)), full((width, width)), pl.BlockSpec((8, 1, n, width), at)],
        12 * 24 * n * width * (span + width),
        scratch=[pltpu.VMEM((8, n, width), jnp.float32)],
        steps=3,
    )


def pack_kernel(ids, trailing, first, second, product, gram, some, columns, vectors, keep, send, rows, piece):
    n, width = first.shape[1:]
    piece[:4] = first[...]
    piece[4:] = second[...]
    last = in_place(ids, piece)
    more_product, more_gram = add_piece(trailing[:, 0], last.reshape(-1, width))
    for x in range(4):
        rows[:, x] = jnp.where(lax.rem(ids[3] + 2, 4) == x, last, some[:, x])
    flat = product[...] + more_product
    sums = gram[...] + more_gram
    projected = dot(vectors[...], rows[...].reshape(-1, width))
    middle = dot(flat, whole(columns, 0, n))
    tall = flat.T
    slab, eig = width // 8, vectors.shape[0]
    mine = ids[1] == 0

    def put(at, low, high):
        size = low.shape[0]
        keep[at : at + size] = jnp.where(mine, low, high)
        send[at : at + size] = jnp.where(mine, high, low)

    for y in range(4):
        at, a, b = y * (n + slab), 2 * y, 2 * y + 1
        put(at, tall[a * n : (a + 1) * n], tall[b * n : (b + 1) * n])
        put(at + n, middle[a * slab : (a + 1) * slab], middle[b * slab : (b + 1) * slab])
    at = 4 * (n + slab)
    put(at, sums[: width // 2], sums[width // 2 :])
    put(at + width // 2, projected[: eig // 2], projected[eig // 2 :])


def pack(ids, trailing, piece, product, gram, rows, columns, vectors):
    n, width = piece[0].shape[1:]
    span = trailing.shape[-1]
    depth = 4 * (n + width // 8) + width // 2 + vectors.shape[0] // 2
    rest = [*piece, product, gram, rows, columns, vectors]
    block = pl.BlockSpec((8, 1, n, span), lambda i, ids: (0, lax.rem(ids[3] + 2, 4), 0, 0))
    shapes = [(depth, width), (depth, width), rows.shape]
    return call(
        pack_kernel,
        ids,
        [trailing, *rest],
        [block] + [full(o.shape) for o in rest],
        [f32(*s) for s in shapes],
        [full(s) for s in shapes],
        12 * width * (8 * n * (span + width) + span * width),
        scratch=[pltpu.VMEM((8, n, width), jnp.float32)],
        grant=WIDE_GRANT,
    )


def route_kernel(ids, keep, got, *outs):
    outs, rest = outs[:-1], outs[-1]
    size = outs[0].shape[0]
    for step, out in enumerate(outs):
        at = pl.ds(pl.multiple_of(lax.rem(ids[0] + step, 4) * size, 8), size)
        out[...] = keep[at] + got[at]
    rest[...] = keep[4 * size :] + got[4 * size :]


def route(ids, keep, got, size):
    depth, width = keep.shape
    shapes = [(size, width)] * 4 + [(depth - 4 * size, width)]
    return call(
        route_kernel,
        ids,
        [keep, got],
        [full(keep.shape)] * 2,
        [f32(*s) for s in shapes],
        [full(s) for s in shapes],
        keep.size,
    )


def settle_kernel(ids, *refs):
    parts, (product, middle) = refs[:4], refs[4:]
    total = parts[0][...] + parts[1][...] + parts[2][...] + parts[3][...]
    n = product.shape[0]
    product[...] = total[:n]
    middle[...] = total[n:]


def settle(ids, parts, n):
    depth, width = parts[0].shape
    shapes = [(n, width), (depth - n, width)]
    return call(
        settle_kernel,
        ids,
        parts,
        [full((depth, width))] * 4,
        [f32(*s) for s in shapes],
        [full(s) for s in shapes],
        1e6,
    )


def spread_kernel(ids, turned, *refs):
    parts, out = refs[:-1], refs[-1]
    n = turned.shape[0]
    middle = parts[0][...] + parts[1][...] + parts[2][...] + parts[3][...]
    for step in range(8):
        out[step, :n] = turned[...]
        out[step, n:] = middle


def spread(ids, turned, parts):
    n, width = turned.shape
    shape = (8, n + parts[0].shape[0], width)
    operands = [turned, *parts]
    return call(
        spread_kernel,
        ids,
        operands,
        [full(o.shape) for o in operands],
        f32(*shape),
        full(shape),
        1e6,
    )


def arrange_kernel(ids, *refs):
    blocks, moved, (first, second, copies) = refs[:9], refs[9], refs[10:]
    half = blocks[4].shape[0]
    for step in range(4):
        first[step] = blocks[step][...]
    second[0, :half] = blocks[4][...]
    second[0, half:] = blocks[5][...]
    for step in range(1, 4):
        second[step] = blocks[step + 5][...]
    for step in range(8):
        copies[step] = moved[...]


def arrange(ids, blocks, moved):
    n, width = moved.shape
    operands = [*blocks, moved]
    shapes = [(4, n, width), (4, n, width), (8, n, width)]
    return call(
        arrange_kernel,
        ids,
        operands,
        [full(o.shape) for o in operands],
        [f32(*s) for s in shapes],
        [full(s) for s in shapes],
        1e6,
    )


def split_kernel(ids, blocks, product, before, first, second, joined):
    n = first.shape[1]
    total = blocks[0, n:]
    for step in range(1, 8):
        total = total + blocks[step, n:]
    first[...] = blocks[:4, :n]
    second[...] = blocks[4:, :n]
    joined[: total.shape[0]] = total
    joined[total.shape[0] :] = product[...]


def split(ids, blocks, product, before):
    _, depth, width = blocks.shape
    n = product.shape[0]
    shapes = [(4, n, width), (4, n, width), (depth, width)]
    return call(
        split_kernel,
        ids,
        [blocks, product, before],
        [full(blocks.shape), full(product.shape), pl.BlockSpec(memory_space=pl.ANY)],
        [f32(*s) for s in shapes],
        [full(s) for s in shapes],
        1e6,
    )


def eliminate(values, scales, factors):
    done = []
    for i, value in enumerate(values):
        for k in range(i):
            value = value - factors[k][i] * done[k]
        done.append(value * scales[i])
    return done

def factor_kernel(ids, own, other, upper, inverse, turns, work):
    n = work.shape[0]
    half, block = n // 2, BLOCK
    low = jnp.where(ids[1] == 0, own[...], other[...])
    high = jnp.where(ids[1] == 0, other[...], own[...])
    work[:half], work[half:] = low[:half], high[:half]
    lane = lax.broadcasted_iota(jnp.int32, (8, half), 1)
    sub = lax.broadcasted_iota(jnp.int32, (8, half), 0)
    spread = lambda v: jnp.broadcast_to(v, (8, half))
    for base in range(0, n, block):
        rest = base + block
        tiles = [[work[base + t : base + t + 8, h * half : (h + 1) * half] for h in (0, 1)] for t in range(0, block, 8)]
        for own in range(block // 8):
            side, at = (base + 8 * own) // half, (base + 8 * own) % half
            tile = tiles[own]
            cols = [spread(tile[side][:, at + k : at + k + 1]) for k in range(8)]
            scales, factors = [], []
            for i in range(8):
                d = spread(cols[i][i : i + 1])
                for k in range(i):
                    d = d - factors[k][i] * factors[k][i]
                scales.append(lax.rsqrt(d))
                line = [None] * 8
                for m in range(i + 1, 8):
                    u = spread(cols[m][i : i + 1])
                    for k in range(i):
                        u = u - factors[k][i] * factors[k][m]
                    line[m] = u * scales[i]
                factors.append(line)
            lines = [[spread(tile[h][k : k + 1]) for k in range(8)] for h in (0, 1)]
            inside = (lane >= at) & (lane < at + 8)
            full = eliminate(lines[side], scales, factors)
            lines[side] = [jnp.where(lane == at + k, 1.0, jnp.where(inside, 0.0, v)) for k, v in enumerate(lines[side])]
            lines = [eliminate(lines[h], scales, factors) for h in (0, 1)]
            for t in range(own + 1, block // 8):
                weights = eliminate([spread(tiles[t][side][:, at + k : at + k + 1]) for k in range(8)], scales, factors)
                for h in (0, 1):
                    value = tiles[t][h]
                    if h == side:
                        value = jnp.where(inside, 0.0, value)
                    for k in range(8):
                        value = value - weights[k] * lines[h][k]
                    tiles[t][h] = value
            for h in (0, 1):
                value = lines[h][0]
                for k in range(1, 8):
                    value = jnp.where(sub == k, lines[h][k], value)
                if h == side:
                    above = full[0]
                    for k in range(1, 8):
                        above = jnp.where(sub == k, full[k], above)
                    value = jnp.where(inside & (lane > at + sub), above, value)
                tile[h] = value
        rows = jnp.concatenate([jnp.concatenate(t, axis=1) for t in tiles], axis=0)
        work[base:rest, :] = rows
        if rest < n:
            wide = lax.broadcasted_iota(jnp.int32, (block, n), 1)
            tall = lax.broadcasted_iota(jnp.int32, (block, n), 0) + base
            lower_rows = jnp.where((wide > tall) & (wide < rest), 0.0, rows)
            change = dot(rows, lower_rows, ((0,), (0,)))
            wide = lax.broadcasted_iota(jnp.int32, (n - rest, n), 1)
            below = jnp.where((wide >= base) & (wide < rest), 0.0, work[rest:, :])
            work[rest:, :] = below - change[rest:, :]
    done = work[...]
    wide = lax.broadcasted_iota(jnp.int32, (n, n), 1)
    tall = lax.broadcasted_iota(jnp.int32, (n, n), 0)
    upper[...] = jnp.where(wide > tall, done, jnp.where(wide == tall, 1.0 / done, 0.0))
    solve = jnp.where(wide <= tall, done, 0.0)
    inverse[...] = solve
    projected = jnp.concatenate([low[half:], high[half:]], axis=0)
    turns[...] = 2.0 * dot(dot(projected, solve, ((1,), (1,))), solve)

def factor(ids, own, other):
    n = own.shape[1]
    shapes = [(n, n), (n, n), (2 * own.shape[0] - n, n)]
    return call(
        factor_kernel,
        ids,
        [own, other],
        [full(own.shape)] * 2,
        [f32(*s) for s in shapes],
        [full(s) for s in shapes],
        1e10,
        scratch=[pltpu.VMEM((n, n), jnp.float32)],
    )


def thirds(x):
    high = x.astype(jnp.bfloat16)
    rest = x - high.astype(jnp.float32)
    middle = rest.astype(jnp.bfloat16)
    return high, middle, (rest - middle.astype(jnp.float32)).astype(jnp.bfloat16)


def six_left(x):
    high, middle, low = thirds(x)
    return jnp.concatenate([high, high, middle, middle, high, low], axis=1)


def six_right(x):
    high, middle, low = thirds(x)
    return jnp.concatenate([high, middle, high, middle, low, high], axis=0)


def times(left, right):
    return jnp.dot(left, right, preferred_element_type=jnp.float32)


def finish_kernel(ids, inverse, columns, turns, vectors, rows, panel, high, middle, rotated, solve):
    @pl.when(pl.program_id(0) == 0)
    def _():
        n = columns.shape[1]
        panel[...] = dot(inverse[...], whole(columns, 0, n), ((1,), (1,)))
        solve[...] = six_right(inverse[...].T)

    high[...], middle[...], _ = thirds(times(six_left(rows[...]), solve[...]))
    rotated[...] = vectors[...] - dot(turns[...], rows[...], ((1,), (1,)))


def finish(ids, inverse, columns, turns, vectors, rows):
    depth, width = rows.shape
    eig = vectors.shape[0]
    span = 8 * columns.shape[1]
    small = [inverse, columns, turns]
    tall = pl.BlockSpec((depth // 4, width), lambda i, ids: (i, 0))
    flat = pl.BlockSpec((eig, depth // 4), lambda i, ids: (0, i))
    wide = full((width, span))
    part = jax.ShapeDtypeStruct((depth, width), jnp.bfloat16)
    return call(
        finish_kernel,
        ids,
        small + [vectors, rows],
        [full(o.shape) for o in small] + [flat, tall],
        [f32(width, span), part, part, f32(eig, depth)],
        [wide, tall, tall, flat],
        12 * width * width * (span + depth),
        scratch=[pltpu.VMEM((6 * width, width), jnp.bfloat16)],
        steps=4,
    )


def couple_kernel(ids, inverse, panel, own, other, right, solve):
    square = inverse[...]
    width, slab = square.shape[0], square.shape[0] // 8
    middle = dot(pick(ids, own, other, 0, slab), square, ((1,), (1,)))
    coupling = dot(square, middle)
    product = dot(square, pick(ids, own, other, slab, own.shape[1]), ((1,), (1,)))
    zeta = 2.0 * product - 2.0 * dot(coupling + coupling.T, panel[...])
    for at, part in ((0, zeta), (width, 2.0 * panel[...])):
        high, middle, _ = thirds(part)
        right[at : at + width] = high
        right[2 * width + at : 3 * width + at] = middle
        right[4 * width + at : 5 * width + at] = high
    solve[...] = six_right(square.T)


def couple(ids, inverse, panel, middles):
    width, span = panel.shape
    operands = [inverse, panel, *middles]
    shapes = [(6 * width, span), (6 * width, width)]
    return call(
        couple_kernel,
        ids,
        operands,
        [full(o.shape) for o in operands],
        [jax.ShapeDtypeStruct(s, jnp.bfloat16) for s in shapes],
        [full(s) for s in shapes],
        12 * (2 * width**3 + 2 * width * width * span),
    )


def update_kernel(count, ids, trailing, basis_high, basis_middle, right, solve, *refs):
    pieces, (out, piece, left) = refs[: 2 * count], refs[-3:]
    width = basis_high.shape[1]
    step = pl.program_id(0)
    for at in range(count):

        @pl.when(step == at)
        def _():
            piece[:4] = pieces[2 * at][...]
            piece[4:] = pieces[2 * at + 1][...]

    rows = times(six_left(piece[...].reshape(-1, width)), solve[...])
    rows_high, rows_middle, _ = thirds(rows)
    parts = ((0, basis_high[...], basis_middle[...]), (width, rows_high, rows_middle))
    for at, high, middle in parts:
        left[:, at : at + width] = high
        left[:, 2 * width + at : 3 * width + at] = high
        left[:, 4 * width + at : 5 * width + at] = middle
    out[...] = trailing[...] - times(left[...], right[...])


def update(ids, trailing, basis, right, solve, pieces, out):
    n, width = pieces[0][0].shape[1:]
    span, count = trailing.shape[1], len(pieces)
    if out is None:
        at = lambda i, ids: (lax.rem(ids[3] + lax.rem(3 * i, 5), 4), 0)
    else:
        at = lambda i, ids: (lax.rem(ids[3] + 2, 4), 0)
    block = pl.BlockSpec((8 * n, span), at)
    rest = [right, solve] + [half for piece in pieces for half in piece]
    operands = [trailing, *basis, *rest]
    in_specs = [block] + [pl.BlockSpec((8 * n, width), at)] * 2 + [full(o.shape) for o in rest]
    aliases = {}
    if out is not None:
        operands.append(out)
        in_specs.append(pl.BlockSpec(memory_space=pl.ANY))
        aliases = {len(operands): 0}
    return call(
        functools.partial(update_kernel, count),
        ids,
        operands,
        in_specs,
        f32(*trailing.shape),
        block,
        6 * count * 8 * n * 2 * width * span,
        aliases,
        [pltpu.VMEM((8, n, width), jnp.float32), pltpu.VMEM((8 * n, 6 * width), jnp.bfloat16)],
        count,
        WIDE_GRANT,
    )


def shards(panel, trailing, vectors):
    n, width = panel.shape
    slab = width // 8
    ids = jnp.stack([lax.axis_index(a) for a in EVERYWHERE]).astype(jnp.int32)
    by_cols = [(c * 8 + r, r * 32 + c) for r in range(8) for c in range(32)]
    turn = [
        (device(y, core, z, x), device(z // 2, z % 2, 2 * y + core, x))
        for y in range(4)
        for core in range(2)
        for z in range(8)
        for x in range(4)
    ]

    moved = lax.ppermute(panel, EVERYWHERE, by_cols)
    first, second, copies = arrange(ids, gather_z(panel), moved)
    own, high, far, low = gather_x(first, second)
    columns = all_to_row(copies)
    cut = trailing.reshape(8, 4, n, -1)
    product, gram, rows = absorb(ids, cut, [own, low, high])
    keep, send, rows = pack(ids, cut, far, product, gram, rows, columns, vectors.T)
    rows = rows.reshape(-1, width)

    *routed, rest = route(ids, keep, swap_core(send), n + slab)
    parts = [routed[0]] + [shift(routed[step], "y", step) for step in (1, 2, 3)]
    own_product, middle = settle(ids, parts, n)
    turned = lax.ppermute(own_product, EVERYWHERE, turn)
    parts = [middle] + [shift(middle, "x", step) for step in (1, 2, 3)]
    rest = rest + sum(shift(rest, "y", step) for step in (1, 2, 3))
    other_rest = swap_core(rest)
    blocks = lax.all_to_all(spread(ids, turned, parts), "z", 0, 0)
    upper, inverse, turns = factor(ids, rest, other_rest)
    panel_cols, high, low, rotated = finish(ids, inverse, columns, turns, vectors.T, rows)
    basis = [high, low]
    first, second, joined = split(ids, blocks, own_product, inverse)
    own, high, far, low = gather_x(first, second)
    right, solve = couple(ids, inverse, panel_cols, gather_row(joined))
    updated = update(ids, trailing, basis, right, solve, [own, low, high], None)
    updated = update(ids, trailing, basis, right, solve, [far], updated)
    return (upper, updated, rotated.T)


def solution(mesh):
    fine = Mesh(mesh.devices.reshape(4, 2, 8, 4), EVERYWHERE)
    row, col = ("y", "core"), ("z", "x")
    return jax.shard_map(
        shards,
        mesh=fine,
        in_specs=(P(row + col, None), P(row, col), P(row, col)),
        out_specs=(P(), P(row, col), P(row, col)),
        check_vma=False,
    )
```

```python
import functools
import jax
import jax.numpy as jnp
from jax import lax
from jax.experimental import pallas as pl
from jax.experimental.pallas import tpu as pltpu
from jax.sharding import Mesh, PartitionSpec as P

EVERYWHERE = ("y", "core", "z", "x")
BLOCK = 64
COST = 0.001
GRANT = 9 * 1024 * 1024
WIDE_GRANT = 48 * 1024 * 1024
UPDATE_GRANT = 30 * 1024 * 1024


def dot(left, right, dims=((1,), (0,))):
    return lax.dot_general(
        left,
        right,
        (dims, ((), ())),
        precision=lax.Precision.HIGHEST,
        preferred_element_type=jnp.float32,
    )


def shift(x, axis, step):
    n = lax.axis_size(axis)
    return lax.ppermute(x, axis, [(i, (i + step) % n) for i in range(n)])


def swap_core(x):
    return lax.ppermute(x, "core", [(0, 1), (1, 0)])


def device(y, core, z, x):
    return ((y * 2 + core) * 8 + z) * 4 + x


def gather_z(x):
    half = x.shape[0] // 2
    low2, high2 = shift(x, "z", 2), shift(x, "z", -2)
    low1, high1 = shift(x, "z", 1), shift(x, "z", -1)
    low3, high3 = shift(low2, "z", 1), shift(high2, "z", -1)
    far = [shift(low2[:half], "z", 2), shift(high2[half:], "z", -2)]
    return [x, high1, high2, high3, *far, low3, low2, low1]


def gather_x(first, second):
    low_a, high_b = shift(first, "x", 1), shift(second, "x", -1)
    low_b, high_a = shift(second, "x", 1), shift(first, "x", -1)
    far = (shift(low_a, "x", 1), shift(high_b, "x", -1))
    return [(first, second), (high_a, high_b), far, (low_a, low_b)]


def all_to_row(copies):
    return lax.all_to_all(copies, ("y", "core"), 0, 0)


def gather_row(x):
    own = jnp.stack([x] + [shift(x, "y", step) for step in (1, 2, 3)])
    return own, swap_core(own)


def pick(ids, own, other, start, stop):
    blocks = []
    for y in range(4):
        place = lax.rem(ids[0] - y + 4, 4)
        for core in (0, 1):
            blocks.append(jnp.where(ids[1] == core, own[place, start:stop], other[place, start:stop]))
    return jnp.concatenate(blocks, axis=0)


def whole(blocks, start, stop):
    return blocks[:, start:stop].reshape(-1, blocks.shape[-1])


def call(
    kernel, ids, operands, in_specs, out_shape, out_specs, flops, aliases=None, scratch=(), steps=1, grant=GRANT
):
    spec = pltpu.PrefetchScalarGridSpec(
        num_scalar_prefetch=1,
        grid=(steps,),
        in_specs=in_specs,
        out_specs=out_specs,
        scratch_shapes=scratch,
    )
    size = sum(o.size * 4 for o in operands[:2])
    return pl.pallas_call(
        kernel,
        grid_spec=spec,
        out_shape=out_shape,
        input_output_aliases=aliases or {},
        cost_estimate=pl.CostEstimate(flops=int(flops * COST), bytes_accessed=int(size * COST), transcendentals=0),
        compiler_params=pltpu.CompilerParams(vmem_limit_bytes=grant),
    )(ids, *operands)


def full(shape):
    return pl.BlockSpec(shape, lambda i, ids: (0,) * len(shape))


def f32(*shape):
    return jax.ShapeDtypeStruct(shape, jnp.float32)


def add_piece(trailing, piece):
    flat = piece.T
    return dot(flat, trailing.reshape(piece.shape[0], -1)), dot(flat, piece)


def in_place(ids, piece):
    return jnp.stack([piece[lax.rem(z - ids[2] + 8, 8)] for z in range(8)])


def absorb_kernel(ids, trailing, *refs):
    pieces, (product, gram, rows, piece) = refs[:6], refs[6:]
    step = pl.program_id(0)
    for at in range(3):

        @pl.when(step == at)
        def _():
            piece[:4] = pieces[2 * at][...]
            piece[4:] = pieces[2 * at + 1][...]

    panel = in_place(ids, piece)
    rows[:, 0] = panel
    more_product, more_gram = add_piece(trailing[:, 0], panel.reshape(-1, panel.shape[-1]))

    @pl.when(step == 0)
    def _():
        product[...], gram[...] = more_product, more_gram

    @pl.when(step > 0)
    def _():
        product[...], gram[...] = product[...] + more_product, gram[...] + more_gram


def absorb(ids, trailing, pieces):
    n, width = pieces[0][0].shape[1:]
    span = trailing.shape[-1]
    at = lambda i, ids: (0, lax.rem(ids[3] + lax.rem(3 * i, 5), 4), 0, 0)
    parts = [half for piece in pieces for half in piece]
    return call(
        absorb_kernel,
        ids,
        [trailing, *parts],
        [pl.BlockSpec((8, 1, n, span), at)] + [full(o.shape) for o in parts],
        [f32(width, span), f32(width, width), f32(8, 4, n, width)],
        [full((width, span)), full((width, width)), pl.BlockSpec((8, 1, n, width), at)],
        12 * 24 * n * width * (span + width),
        scratch=[pltpu.VMEM((8, n, width), jnp.float32)],
        steps=3,
    )


def pack_kernel(ids, trailing, first, second, product, gram, some, columns, vectors, keep, send, rows, piece):
    n, width = first.shape[1:]
    piece[:4] = first[...]
    piece[4:] = second[...]
    last = in_place(ids, piece)
    more_product, more_gram = add_piece(trailing[:, 0], last.reshape(-1, width))
    for x in range(4):
        rows[:, x] = jnp.where(lax.rem(ids[3] + 2, 4) == x, last, some[:, x])
    flat = product[...] + more_product
    sums = gram[...] + more_gram
    projected = dot(vectors[...], rows[...].reshape(-1, width))
    middle = dot(flat, whole(columns, 0, n))
    tall = flat.T
    slab, eig = width // 8, vectors.shape[0]
    mine = ids[1] == 0

    def put(at, low, high):
        size = low.shape[0]
        keep[at : at + size] = jnp.where(mine, low, high)
        send[at : at + size] = jnp.where(mine, high, low)

    for y in range(4):
        at, a, b = y * (n + slab), 2 * y, 2 * y + 1
        put(at, tall[a * n : (a + 1) * n], tall[b * n : (b + 1) * n])
        put(at + n, middle[a * slab : (a + 1) * slab], middle[b * slab : (b + 1) * slab])
    at = 4 * (n + slab)
    put(at, sums[: width // 2], sums[width // 2 :])
    put(at + width // 2, projected[: eig // 2], projected[eig // 2 :])


def pack(ids, trailing, piece, product, gram, rows, columns, vectors):
    n, width = piece[0].shape[1:]
    span = trailing.shape[-1]
    depth = 4 * (n + width // 8) + width // 2 + vectors.shape[0] // 2
    rest = [*piece, product, gram, rows, columns, vectors]
    block = pl.BlockSpec((8, 1, n, span), lambda i, ids: (0, lax.rem(ids[3] + 2, 4), 0, 0))
    shapes = [(depth, width), (depth, width), rows.shape]
    return call(
        pack_kernel,
        ids,
        [trailing, *rest],
        [block] + [full(o.shape) for o in rest],
        [f32(*s) for s in shapes],
        [full(s) for s in shapes],
        12 * width * (8 * n * (span + width) + span * width),
        scratch=[pltpu.VMEM((8, n, width), jnp.float32)],
        grant=WIDE_GRANT,
    )


def route_kernel(ids, keep, got, *outs):
    outs, rest = outs[:-1], outs[-1]
    size = outs[0].shape[0]
    for step, out in enumerate(outs):
        at = pl.ds(pl.multiple_of(lax.rem(ids[0] + step, 4) * size, 8), size)
        out[...] = keep[at] + got[at]
    rest[...] = keep[4 * size :] + got[4 * size :]


def route(ids, keep, got, size):
    depth, width = keep.shape
    shapes = [(size, width)] * 4 + [(depth - 4 * size, width)]
    return call(
        route_kernel,
        ids,
        [keep, got],
        [full(keep.shape)] * 2,
        [f32(*s) for s in shapes],
        [full(s) for s in shapes],
        keep.size,
    )


def settle_kernel(ids, *refs):
    parts, (product, middle) = refs[:4], refs[4:]
    total = parts[0][...] + parts[1][...] + parts[2][...] + parts[3][...]
    n = product.shape[0]
    product[...] = total[:n]
    middle[...] = total[n:]


def settle(ids, parts, n):
    depth, width = parts[0].shape
    shapes = [(n, width), (depth - n, width)]
    return call(
        settle_kernel,
        ids,
        parts,
        [full((depth, width))] * 4,
        [f32(*s) for s in shapes],
        [full(s) for s in shapes],
        1e6,
    )


def spread_kernel(ids, turned, *refs):
    parts, out = refs[:-1], refs[-1]
    n = turned.shape[0]
    middle = parts[0][...] + parts[1][...] + parts[2][...] + parts[3][...]
    for step in range(8):
        out[step, :n] = turned[...]
        out[step, n:] = middle


def spread(ids, turned, parts):
    n, width = turned.shape
    shape = (8, n + parts[0].shape[0], width)
    operands = [turned, *parts]
    return call(
        spread_kernel,
        ids,
        operands,
        [full(o.shape) for o in operands],
        f32(*shape),
        full(shape),
        1e6,
    )


def arrange_kernel(ids, *refs):
    blocks, moved, (first, second, copies) = refs[:9], refs[9], refs[10:]
    half = blocks[4].shape[0]
    for step in range(4):
        first[step] = blocks[step][...]
    second[0, :half] = blocks[4][...]
    second[0, half:] = blocks[5][...]
    for step in range(1, 4):
        second[step] = blocks[step + 5][...]
    for step in range(8):
        copies[step] = moved[...]


def arrange(ids, blocks, moved):
    n, width = moved.shape
    operands = [*blocks, moved]
    shapes = [(4, n, width), (4, n, width), (8, n, width)]
    return call(
        arrange_kernel,
        ids,
        operands,
        [full(o.shape) for o in operands],
        [f32(*s) for s in shapes],
        [full(s) for s in shapes],
        1e6,
    )


def split_kernel(ids, blocks, product, before, first, second, joined):
    n = first.shape[1]
    total = blocks[0, n:]
    for step in range(1, 8):
        total = total + blocks[step, n:]
    first[...] = blocks[:4, :n]
    second[...] = blocks[4:, :n]
    joined[: total.shape[0]] = total
    joined[total.shape[0] :] = product[...]


def split(ids, blocks, product, before):
    _, depth, width = blocks.shape
    n = product.shape[0]
    shapes = [(4, n, width), (4, n, width), (depth, width)]
    return call(
        split_kernel,
        ids,
        [blocks, product, before],
        [full(blocks.shape), full(product.shape), pl.BlockSpec(memory_space=pl.ANY)],
        [f32(*s) for s in shapes],
        [full(s) for s in shapes],
        1e6,
    )


def eliminate(values, scales, factors):
    done = []
    for i, value in enumerate(values):
        for k in range(i):
            value = value - factors[k][i] * done[k]
        done.append(value * scales[i])
    return done

def factor_kernel(ids, own, other, upper, inverse, turns, work):
    n = work.shape[0]
    half, block = n // 2, BLOCK
    low = jnp.where(ids[1] == 0, own[...], other[...])
    high = jnp.where(ids[1] == 0, other[...], own[...])
    work[:half], work[half:] = low[:half], high[:half]
    lane = lax.broadcasted_iota(jnp.int32, (8, half), 1)
    sub = lax.broadcasted_iota(jnp.int32, (8, half), 0)
    spread = lambda v: jnp.broadcast_to(v, (8, half))
    for base in range(0, n, block):
        rest = base + block
        tiles = [[work[base + t : base + t + 8, h * half : (h + 1) * half] for h in (0, 1)] for t in range(0, block, 8)]
        for own in range(block // 8):
            side, at = (base + 8 * own) // half, (base + 8 * own) % half
            tile = tiles[own]
            cols = [spread(tile[side][:, at + k : at + k + 1]) for k in range(8)]
            scales, factors = [], []
            for i in range(8):
                d = spread(cols[i][i : i + 1])
                for k in range(i):
                    d = d - factors[k][i] * factors[k][i]
                scales.append(lax.rsqrt(d))
                line = [None] * 8
                for m in range(i + 1, 8):
                    u = spread(cols[m][i : i + 1])
                    for k in range(i):
                        u = u - factors[k][i] * factors[k][m]
                    line[m] = u * scales[i]
                factors.append(line)
            lines = [[spread(tile[h][k : k + 1]) for k in range(8)] for h in (0, 1)]
            inside = (lane >= at) & (lane < at + 8)
            full = eliminate(lines[side], scales, factors)
            lines[side] = [jnp.where(lane == at + k, 1.0, jnp.where(inside, 0.0, v)) for k, v in enumerate(lines[side])]
            lines = [eliminate(lines[h], scales, factors) for h in (0, 1)]
            for t in range(own + 1, block // 8):
                weights = eliminate([spread(tiles[t][side][:, at + k : at + k + 1]) for k in range(8)], scales, factors)
                for h in (0, 1):
                    value = tiles[t][h]
                    if h == side:
                        value = jnp.where(inside, 0.0, value)
                    for k in range(8):
                        value = value - weights[k] * lines[h][k]
                    tiles[t][h] = value
            for h in (0, 1):
                value = lines[h][0]
                for k in range(1, 8):
                    value = jnp.where(sub == k, lines[h][k], value)
                if h == side:
                    above = full[0]
                    for k in range(1, 8):
                        above = jnp.where(sub == k, full[k], above)
                    value = jnp.where(inside & (lane > at + sub), above, value)
                tile[h] = value
        rows = jnp.concatenate([jnp.concatenate(t, axis=1) for t in tiles], axis=0)
        work[base:rest, :] = rows
        if rest < n:
            wide = lax.broadcasted_iota(jnp.int32, (block, n), 1)
            tall = lax.broadcasted_iota(jnp.int32, (block, n), 0) + base
            lower_rows = jnp.where((wide > tall) & (wide < rest), 0.0, rows)
            change = dot(rows, lower_rows, ((0,), (0,)))
            wide = lax.broadcasted_iota(jnp.int32, (n - rest, n), 1)
            below = jnp.where((wide >= base) & (wide < rest), 0.0, work[rest:, :])
            work[rest:, :] = below - change[rest:, :]
    done = work[...]
    wide = lax.broadcasted_iota(jnp.int32, (n, n), 1)
    tall = lax.broadcasted_iota(jnp.int32, (n, n), 0)
    upper[...] = jnp.where(wide > tall, done, jnp.where(wide == tall, 1.0 / done, 0.0))
    solve = jnp.where(wide <= tall, done, 0.0)
    inverse[...] = solve
    projected = jnp.concatenate([low[half:], high[half:]], axis=0)
    turns[...] = 2.0 * dot(dot(projected, solve, ((1,), (1,))), solve)

def factor(ids, own, other):
    n = own.shape[1]
    shapes = [(n, n), (n, n), (2 * own.shape[0] - n, n)]
    return call(
        factor_kernel,
        ids,
        [own, other],
        [full(own.shape)] * 2,
        [f32(*s) for s in shapes],
        [full(s) for s in shapes],
        1e10,
        scratch=[pltpu.VMEM((n, n), jnp.float32)],
    )


def thirds(x):
    high = x.astype(jnp.bfloat16)
    rest = x - high.astype(jnp.float32)
    middle = rest.astype(jnp.bfloat16)
    return high, middle, (rest - middle.astype(jnp.float32)).astype(jnp.bfloat16)


def six_left(x):
    high, middle, low = thirds(x)
    return jnp.concatenate([high, high, middle, middle, high, low], axis=1)


def six_right(x):
    high, middle, low = thirds(x)
    return jnp.concatenate([high, middle, high, middle, low, high], axis=0)


def times(left, right):
    return jnp.dot(left, right, preferred_element_type=jnp.float32)


def finish_kernel(ids, inverse, columns, turns, vectors, rows, panel, high, middle, rotated, solve):
    @pl.when(pl.program_id(0) == 0)
    def _():
        n = columns.shape[1]
        panel[...] = dot(inverse[...], whole(columns, 0, n), ((1,), (1,)))
        solve[...] = six_right(inverse[...].T)

    high[...], middle[...], _ = thirds(times(six_left(rows[...]), solve[...]))
    rotated[...] = vectors[...] - dot(turns[...], rows[...], ((1,), (1,)))


def finish(ids, inverse, columns, turns, vectors, rows):
    depth, width = rows.shape
    eig = vectors.shape[0]
    span = 8 * columns.shape[1]
    small = [inverse, columns, turns]
    tall = pl.BlockSpec((depth // 4, width), lambda i, ids: (i, 0))
    flat = pl.BlockSpec((eig, depth // 4), lambda i, ids: (0, i))
    wide = full((width, span))
    part = jax.ShapeDtypeStruct((depth, width), jnp.bfloat16)
    return call(
        finish_kernel,
        ids,
        small + [vectors, rows],
        [full(o.shape) for o in small] + [flat, tall],
        [f32(width, span), part, part, f32(eig, depth)],
        [wide, tall, tall, flat],
        12 * width * width * (span + depth),
        scratch=[pltpu.VMEM((6 * width, width), jnp.bfloat16)],
        steps=4,
    )


def couple_kernel(ids, inverse, panel, own, other, right, solve):
    square = inverse[...]
    width, slab = square.shape[0], square.shape[0] // 8
    middle = dot(pick(ids, own, other, 0, slab), square, ((1,), (1,)))
    coupling = dot(square, middle)
    product = dot(square, pick(ids, own, other, slab, own.shape[1]), ((1,), (1,)))
    zeta = 2.0 * product - 2.0 * dot(coupling + coupling.T, panel[...])
    for at, part in ((0, zeta), (width, 2.0 * panel[...])):
        high, middle, _ = thirds(part)
        right[at : at + width] = high
        right[2 * width + at : 3 * width + at] = middle
        right[4 * width + at : 5 * width + at] = high
    solve[...] = six_right(square.T)


def couple(ids, inverse, panel, middles):
    width, span = panel.shape
    operands = [inverse, panel, *middles]
    shapes = [(6 * width, span), (6 * width, width)]
    return call(
        couple_kernel,
        ids,
        operands,
        [full(o.shape) for o in operands],
        [jax.ShapeDtypeStruct(s, jnp.bfloat16) for s in shapes],
        [full(s) for s in shapes],
        12 * (2 * width**3 + 2 * width * width * span),
    )


def update_kernel(count, ids, trailing, basis_high, basis_middle, right, solve, *refs):
    pieces, (out, piece, left) = refs[: 2 * count], refs[-3:]
    width = basis_high.shape[1]
    step = pl.program_id(0)
    for at in range(count):

        @pl.when(step == at)
        def _():
            piece[:4] = pieces[2 * at][...]
            piece[4:] = pieces[2 * at + 1][...]

    rows = times(six_left(piece[...].reshape(-1, width)), solve[...])
    rows_high, rows_middle, _ = thirds(rows)
    parts = ((0, basis_high[...], basis_middle[...]), (width, rows_high, rows_middle))
    for at, high, middle in parts:
        left[:, at : at + width] = high
        left[:, 2 * width + at : 3 * width + at] = high
        left[:, 4 * width + at : 5 * width + at] = middle
    out[...] = trailing[...] - times(left[...], right[...])


def update(ids, trailing, basis, right, solve, pieces, out):
    n, width = pieces[0][0].shape[1:]
    span, count = trailing.shape[1], len(pieces)
    if out is None:
        at = lambda i, ids: (lax.rem(ids[3] + lax.rem(3 * i, 5), 4), 0)
    else:
        at = lambda i, ids: (lax.rem(ids[3] + 2, 4), 0)
    block = pl.BlockSpec((8 * n, span), at)
    rest = [right, solve] + [half for piece in pieces for half in piece]
    operands = [trailing, *basis, *rest]
    in_specs = [block] + [pl.BlockSpec((8 * n, width), at)] * 2 + [full(o.shape) for o in rest]
    aliases = {}
    if out is not None:
        operands.append(out)
        in_specs.append(pl.BlockSpec(memory_space=pl.ANY))
        aliases = {len(operands): 0}
    return call(
        functools.partial(update_kernel, count),
        ids,
        operands,
        in_specs,
        f32(*trailing.shape),
        block,
        6 * count * 8 * n * 2 * width * span,
        aliases,
        [pltpu.VMEM((8, n, width), jnp.float32), pltpu.VMEM((8 * n, 6 * width), jnp.bfloat16)],
        count,
        UPDATE_GRANT,
    )


def shards(panel, trailing, vectors):
    n, width = panel.shape
    slab = width // 8
    ids = jnp.stack([lax.axis_index(a) for a in EVERYWHERE]).astype(jnp.int32)
    by_cols = [(c * 8 + r, r * 32 + c) for r in range(8) for c in range(32)]
    turn = [
        (device(y, core, z, x), device(z // 2, z % 2, 2 * y + core, x))
        for y in range(4)
        for core in range(2)
        for z in range(8)
        for x in range(4)
    ]

    moved = lax.ppermute(panel, EVERYWHERE, by_cols)
    first, second, copies = arrange(ids, gather_z(panel), moved)
    own, high, far, low = gather_x(first, second)
    columns = all_to_row(copies)
    cut = trailing.reshape(8, 4, n, -1)
    product, gram, rows = absorb(ids, cut, [own, low, high])
    keep, send, rows = pack(ids, cut, far, product, gram, rows, columns, vectors.T)
    rows = rows.reshape(-1, width)

    *routed, rest = route(ids, keep, swap_core(send), n + slab)
    parts = [routed[0]] + [shift(routed[step], "y", step) for step in (1, 2, 3)]
    own_product, middle = settle(ids, parts, n)
    turned = lax.ppermute(own_product, EVERYWHERE, turn)
    parts = [middle] + [shift(middle, "x", step) for step in (1, 2, 3)]
    rest = rest + sum(shift(rest, "y", step) for step in (1, 2, 3))
    other_rest = swap_core(rest)
    blocks = lax.all_to_all(spread(ids, turned, parts), "z", 0, 0)
    upper, inverse, turns = factor(ids, rest, other_rest)
    panel_cols, high, low, rotated = finish(ids, inverse, columns, turns, vectors.T, rows)
    basis = [high, low]
    first, second, joined = split(ids, blocks, own_product, inverse)
    own, high, far, low = gather_x(first, second)
    right, solve = couple(ids, inverse, panel_cols, gather_row(joined))
    updated = update(ids, trailing, basis, right, solve, [own, low, high], None)
    updated = update(ids, trailing, basis, right, solve, [far], updated)
    return (upper, updated, rotated.T)


def solution(mesh):
    fine = Mesh(mesh.devices.reshape(4, 2, 8, 4), EVERYWHERE)
    row, col = ("y", "core"), ("z", "x")
    return jax.shard_map(
        shards,
        mesh=fine,
        in_specs=(P(row + col, None), P(row, col), P(row, col)),
        out_specs=(P(), P(row, col), P(row, col)),
        check_vma=False,
    )
```

```python
import functools
import jax
import jax.numpy as jnp
from jax import lax
from jax.experimental import pallas as pl
from jax.experimental.pallas import tpu as pltpu
from jax.sharding import Mesh, PartitionSpec as P

EVERYWHERE = ("y", "core", "z", "x")
BLOCK = 64
COST = 0.001
GRANT = 9 * 1024 * 1024
WIDE_GRANT = 48 * 1024 * 1024
UPDATE_GRANT = 30 * 1024 * 1024


def dot(left, right, dims=((1,), (0,))):
    return lax.dot_general(
        left,
        right,
        (dims, ((), ())),
        precision=lax.Precision.HIGHEST,
        preferred_element_type=jnp.float32,
    )


def shift(x, axis, step):
    n = lax.axis_size(axis)
    return lax.ppermute(x, axis, [(i, (i + step) % n) for i in range(n)])


def swap_core(x):
    return lax.ppermute(x, "core", [(0, 1), (1, 0)])


def device(y, core, z, x):
    return ((y * 2 + core) * 8 + z) * 4 + x


def gather_z(x):
    half = x.shape[0] // 2
    low2, high2 = shift(x, "z", 2), shift(x, "z", -2)
    low1, high1 = shift(x, "z", 1), shift(x, "z", -1)
    low3, high3 = shift(low2, "z", 1), shift(high2, "z", -1)
    far = [shift(low2[:half], "z", 2), shift(high2[half:], "z", -2)]
    return [x, high1, high2, high3, *far, low3, low2, low1]


def gather_x(first, second):
    low_a, high_b = shift(first, "x", 1), shift(second, "x", -1)
    low_b, high_a = shift(second, "x", 1), shift(first, "x", -1)
    far = (shift(low_a, "x", 1), shift(high_b, "x", -1))
    return [(first, second), (high_a, high_b), far, (low_a, low_b)]


def all_to_row(copies):
    return lax.all_to_all(copies, ("y", "core"), 0, 0)


def gather_row(x):
    own = jnp.stack([x] + [shift(x, "y", step) for step in (1, 2, 3)])
    return own, swap_core(own)


def pick(ids, own, other, start, stop):
    blocks = []
    for y in range(4):
        place = lax.rem(ids[0] - y + 4, 4)
        for core in (0, 1):
            blocks.append(jnp.where(ids[1] == core, own[place, start:stop], other[place, start:stop]))
    return jnp.concatenate(blocks, axis=0)


def whole(blocks, start, stop):
    return blocks[:, start:stop].reshape(-1, blocks.shape[-1])


def call(
    kernel, ids, operands, in_specs, out_shape, out_specs, flops, aliases=None, scratch=(), steps=1, grant=GRANT
):
    spec = pltpu.PrefetchScalarGridSpec(
        num_scalar_prefetch=1,
        grid=(steps,),
        in_specs=in_specs,
        out_specs=out_specs,
        scratch_shapes=scratch,
    )
    size = sum(o.size * 4 for o in operands[:2])
    return pl.pallas_call(
        kernel,
        grid_spec=spec,
        out_shape=out_shape,
        input_output_aliases=aliases or {},
        cost_estimate=pl.CostEstimate(flops=int(flops * COST), bytes_accessed=int(size * COST), transcendentals=0),
        compiler_params=pltpu.CompilerParams(vmem_limit_bytes=grant),
    )(ids, *operands)


def full(shape):
    return pl.BlockSpec(shape, lambda i, ids: (0,) * len(shape))


def f32(*shape):
    return jax.ShapeDtypeStruct(shape, jnp.float32)


def add_piece(trailing, piece):
    flat = piece.T
    return dot(flat, trailing.reshape(piece.shape[0], -1)), dot(flat, piece)


def in_place(ids, piece):
    return jnp.stack([piece[lax.rem(z - ids[2] + 8, 8)] for z in range(8)])


def absorb_kernel(ids, trailing, *refs):
    pieces, (product, gram, rows, piece) = refs[:6], refs[6:]
    step = pl.program_id(0)
    for at in range(3):

        @pl.when(step == at)
        def _():
            piece[:4] = pieces[2 * at][...]
            piece[4:] = pieces[2 * at + 1][...]

    panel = in_place(ids, piece)
    rows[:, 0] = panel
    more_product, more_gram = add_piece(trailing[:, 0], panel.reshape(-1, panel.shape[-1]))

    @pl.when(step == 0)
    def _():
        product[...], gram[...] = more_product, more_gram

    @pl.when(step > 0)
    def _():
        product[...], gram[...] = product[...] + more_product, gram[...] + more_gram


def absorb(ids, trailing, pieces):
    n, width = pieces[0][0].shape[1:]
    span = trailing.shape[-1]
    at = lambda i, ids: (0, lax.rem(ids[3] + lax.rem(3 * i, 5), 4), 0, 0)
    parts = [half for piece in pieces for half in piece]
    return call(
        absorb_kernel,
        ids,
        [trailing, *parts],
        [pl.BlockSpec((8, 1, n, span), at)] + [full(o.shape) for o in parts],
        [f32(width, span), f32(width, width), f32(8, 4, n, width)],
        [full((width, span)), full((width, width)), pl.BlockSpec((8, 1, n, width), at)],
        12 * 24 * n * width * (span + width),
        scratch=[pltpu.VMEM((8, n, width), jnp.float32)],
        steps=3,
    )


def pack_kernel(ids, trailing, first, second, product, gram, some, columns, vectors, keep, send, rows, piece):
    n, width = first.shape[1:]
    piece[:4] = first[...]
    piece[4:] = second[...]
    last = in_place(ids, piece)
    more_product, more_gram = add_piece(trailing[:, 0], last.reshape(-1, width))
    for x in range(4):
        rows[:, x] = jnp.where(lax.rem(ids[3] + 2, 4) == x, last, some[:, x])
    flat = product[...] + more_product
    sums = gram[...] + more_gram
    projected = dot(vectors[...], rows[...].reshape(-1, width))
    middle = dot(flat, whole(columns, 0, n))
    tall = flat.T
    slab, eig = width // 8, vectors.shape[0]
    mine = ids[1] == 0

    def put(at, low, high):
        size = low.shape[0]
        keep[at : at + size] = jnp.where(mine, low, high)
        send[at : at + size] = jnp.where(mine, high, low)

    for y in range(4):
        at, a, b = y * (n + slab), 2 * y, 2 * y + 1
        put(at, tall[a * n : (a + 1) * n], tall[b * n : (b + 1) * n])
        put(at + n, middle[a * slab : (a + 1) * slab], middle[b * slab : (b + 1) * slab])
    at = 4 * (n + slab)
    put(at, sums[: width // 2], sums[width // 2 :])
    put(at + width // 2, projected[: eig // 2], projected[eig // 2 :])


def pack(ids, trailing, piece, product, gram, rows, columns, vectors):
    n, width = piece[0].shape[1:]
    span = trailing.shape[-1]
    depth = 4 * (n + width // 8) + width // 2 + vectors.shape[0] // 2
    rest = [*piece, product, gram, rows, columns, vectors]
    block = pl.BlockSpec((8, 1, n, span), lambda i, ids: (0, lax.rem(ids[3] + 2, 4), 0, 0))
    shapes = [(depth, width), (depth, width), rows.shape]
    return call(
        pack_kernel,
        ids,
        [trailing, *rest],
        [block] + [full(o.shape) for o in rest],
        [f32(*s) for s in shapes],
        [full(s) for s in shapes],
        12 * width * (8 * n * (span + width) + span * width),
        scratch=[pltpu.VMEM((8, n, width), jnp.float32)],
        grant=WIDE_GRANT,
    )


def route_kernel(ids, keep, got, *outs):
    outs, rest = outs[:-1], outs[-1]
    size = outs[0].shape[0]
    for step, out in enumerate(outs):
        at = pl.ds(pl.multiple_of(lax.rem(ids[0] + step, 4) * size, 8), size)
        out[...] = keep[at] + got[at]
    rest[...] = keep[4 * size :] + got[4 * size :]


def route(ids, keep, got, size):
    depth, width = keep.shape
    shapes = [(size, width)] * 4 + [(depth - 4 * size, width)]
    return call(
        route_kernel,
        ids,
        [keep, got],
        [full(keep.shape)] * 2,
        [f32(*s) for s in shapes],
        [full(s) for s in shapes],
        keep.size,
    )


def settle_kernel(ids, *refs):
    parts, (product, middle) = refs[:4], refs[4:]
    total = parts[0][...] + parts[1][...] + parts[2][...] + parts[3][...]
    n = product.shape[0]
    product[...] = total[:n]
    middle[...] = total[n:]


def settle(ids, parts, n):
    depth, width = parts[0].shape
    shapes = [(n, width), (depth - n, width)]
    return call(
        settle_kernel,
        ids,
        parts,
        [full((depth, width))] * 4,
        [f32(*s) for s in shapes],
        [full(s) for s in shapes],
        1e6,
    )


def spread_kernel(ids, turned, *refs):
    parts, out = refs[:-1], refs[-1]
    n = turned.shape[0]
    middle = parts[0][...] + parts[1][...] + parts[2][...] + parts[3][...]
    for step in range(8):
        out[step, :n] = turned[...]
        out[step, n:] = middle


def spread(ids, turned, parts):
    n, width = turned.shape
    shape = (8, n + parts[0].shape[0], width)
    operands = [turned, *parts]
    return call(
        spread_kernel,
        ids,
        operands,
        [full(o.shape) for o in operands],
        f32(*shape),
        full(shape),
        1e6,
    )


def arrange_kernel(ids, *refs):
    blocks, moved, (first, second, copies) = refs[:9], refs[9], refs[10:]
    half = blocks[4].shape[0]
    for step in range(4):
        first[step] = blocks[step][...]
    second[0, :half] = blocks[4][...]
    second[0, half:] = blocks[5][...]
    for step in range(1, 4):
        second[step] = blocks[step + 5][...]
    for step in range(8):
        copies[step] = moved[...]


def arrange(ids, blocks, moved):
    n, width = moved.shape
    operands = [*blocks, moved]
    shapes = [(4, n, width), (4, n, width), (8, n, width)]
    return call(
        arrange_kernel,
        ids,
        operands,
        [full(o.shape) for o in operands],
        [f32(*s) for s in shapes],
        [full(s) for s in shapes],
        1e6,
    )


def split_kernel(ids, blocks, product, before, own, joined):
    n = own.shape[1]
    total = blocks[0, n:]
    for step in range(1, 8):
        total = total + blocks[step, n:]
    own[...] = blocks[:, :n]
    joined[: total.shape[0]] = total
    joined[total.shape[0] :] = product[...]


def split(ids, blocks, product, before):
    _, depth, width = blocks.shape
    n = product.shape[0]
    shapes = [(8, n, width), (depth, width)]
    return call(
        split_kernel,
        ids,
        [blocks, product, before],
        [full(blocks.shape), full(product.shape), pl.BlockSpec(memory_space=pl.ANY)],
        [f32(*s) for s in shapes],
        [full(s) for s in shapes],
        1e6,
    )


def eliminate(values, scales, factors):
    done = []
    for i, value in enumerate(values):
        for k in range(i):
            value = value - factors[k][i] * done[k]
        done.append(value * scales[i])
    return done

def factor_kernel(ids, own, other, upper, inverse, turns, work):
    n = work.shape[0]
    half, block = n // 2, BLOCK
    low = jnp.where(ids[1] == 0, own[...], other[...])
    high = jnp.where(ids[1] == 0, other[...], own[...])
    work[:half], work[half:] = low[:half], high[:half]
    lane = lax.broadcasted_iota(jnp.int32, (8, half), 1)
    sub = lax.broadcasted_iota(jnp.int32, (8, half), 0)
    spread = lambda v: jnp.broadcast_to(v, (8, half))
    for base in range(0, n, block):
        rest = base + block
        tiles = [[work[base + t : base + t + 8, h * half : (h + 1) * half] for h in (0, 1)] for t in range(0, block, 8)]
        for own in range(block // 8):
            side, at = (base + 8 * own) // half, (base + 8 * own) % half
            tile = tiles[own]
            cols = [spread(tile[side][:, at + k : at + k + 1]) for k in range(8)]
            scales, factors = [], []
            for i in range(8):
                d = spread(cols[i][i : i + 1])
                for k in range(i):
                    d = d - factors[k][i] * factors[k][i]
                scales.append(lax.rsqrt(d))
                line = [None] * 8
                for m in range(i + 1, 8):
                    u = spread(cols[m][i : i + 1])
                    for k in range(i):
                        u = u - factors[k][i] * factors[k][m]
                    line[m] = u * scales[i]
                factors.append(line)
            lines = [[spread(tile[h][k : k + 1]) for k in range(8)] for h in (0, 1)]
            inside = (lane >= at) & (lane < at + 8)
            full = eliminate(lines[side], scales, factors)
            lines[side] = [jnp.where(lane == at + k, 1.0, jnp.where(inside, 0.0, v)) for k, v in enumerate(lines[side])]
            lines = [eliminate(lines[h], scales, factors) for h in (0, 1)]
            for t in range(own + 1, block // 8):
                weights = eliminate([spread(tiles[t][side][:, at + k : at + k + 1]) for k in range(8)], scales, factors)
                for h in (0, 1):
                    value = tiles[t][h]
                    if h == side:
                        value = jnp.where(inside, 0.0, value)
                    for k in range(8):
                        value = value - weights[k] * lines[h][k]
                    tiles[t][h] = value
            for h in (0, 1):
                value = lines[h][0]
                for k in range(1, 8):
                    value = jnp.where(sub == k, lines[h][k], value)
                if h == side:
                    above = full[0]
                    for k in range(1, 8):
                        above = jnp.where(sub == k, full[k], above)
                    value = jnp.where(inside & (lane > at + sub), above, value)
                tile[h] = value
        rows = jnp.concatenate([jnp.concatenate(t, axis=1) for t in tiles], axis=0)
        work[base:rest, :] = rows
        if rest < n:
            wide = lax.broadcasted_iota(jnp.int32, (block, n), 1)
            tall = lax.broadcasted_iota(jnp.int32, (block, n), 0) + base
            lower_rows = jnp.where((wide > tall) & (wide < rest), 0.0, rows)
            change = dot(rows, lower_rows, ((0,), (0,)))
            wide = lax.broadcasted_iota(jnp.int32, (n - rest, n), 1)
            below = jnp.where((wide >= base) & (wide < rest), 0.0, work[rest:, :])
            work[rest:, :] = below - change[rest:, :]
    done = work[...]
    wide = lax.broadcasted_iota(jnp.int32, (n, n), 1)
    tall = lax.broadcasted_iota(jnp.int32, (n, n), 0)
    upper[...] = jnp.where(wide > tall, done, jnp.where(wide == tall, 1.0 / done, 0.0))
    solve = jnp.where(wide <= tall, done, 0.0)
    inverse[...] = solve
    projected = jnp.concatenate([low[half:], high[half:]], axis=0)
    turns[...] = 2.0 * dot(dot(projected, solve, ((1,), (1,))), solve)

def factor(ids, own, other):
    n = own.shape[1]
    shapes = [(n, n), (n, n), (2 * own.shape[0] - n, n)]
    return call(
        factor_kernel,
        ids,
        [own, other],
        [full(own.shape)] * 2,
        [f32(*s) for s in shapes],
        [full(s) for s in shapes],
        1e10,
        scratch=[pltpu.VMEM((n, n), jnp.float32)],
    )


def thirds(x):
    high = x.astype(jnp.bfloat16)
    rest = x - high.astype(jnp.float32)
    middle = rest.astype(jnp.bfloat16)
    return high, middle, (rest - middle.astype(jnp.float32)).astype(jnp.bfloat16)


def six_left(x):
    high, middle, low = thirds(x)
    return jnp.concatenate([high, high, middle, middle, high, low], axis=1)


def six_right(x):
    high, middle, low = thirds(x)
    return jnp.concatenate([high, middle, high, middle, low, high], axis=0)


def times(left, right):
    return jnp.dot(left, right, preferred_element_type=jnp.float32)


def finish_kernel(ids, inverse, columns, turns, vectors, rows, panel, high, middle, rotated, solve):
    @pl.when(pl.program_id(0) == 0)
    def _():
        n = columns.shape[1]
        panel[...] = dot(inverse[...], whole(columns, 0, n), ((1,), (1,)))
        solve[...] = six_right(inverse[...].T)

    high[...], middle[...], _ = thirds(times(six_left(rows[...]), solve[...]))
    rotated[...] = vectors[...] - dot(turns[...], rows[...], ((1,), (1,)))


def finish(ids, inverse, columns, turns, vectors, rows):
    depth, width = rows.shape
    eig = vectors.shape[0]
    span = 8 * columns.shape[1]
    small = [inverse, columns, turns]
    tall = pl.BlockSpec((depth // 4, width), lambda i, ids: (i, 0))
    flat = pl.BlockSpec((eig, depth // 4), lambda i, ids: (0, i))
    wide = full((width, span))
    part = jax.ShapeDtypeStruct((depth, width), jnp.bfloat16)
    return call(
        finish_kernel,
        ids,
        small + [vectors, rows],
        [full(o.shape) for o in small] + [flat, tall],
        [f32(width, span), part, part, f32(eig, depth)],
        [wide, tall, tall, flat],
        12 * width * width * (span + depth),
        scratch=[pltpu.VMEM((6 * width, width), jnp.bfloat16)],
        steps=4,
    )


def couple_kernel(ids, inverse, panel, own, other, right, solve):
    square = inverse[...]
    width, slab = square.shape[0], square.shape[0] // 8
    middle = dot(pick(ids, own, other, 0, slab), square, ((1,), (1,)))
    coupling = dot(square, middle)
    product = dot(square, pick(ids, own, other, slab, own.shape[1]), ((1,), (1,)))
    zeta = 2.0 * product - 2.0 * dot(coupling + coupling.T, panel[...])
    for at, part in ((0, zeta), (width, 2.0 * panel[...])):
        high, middle, _ = thirds(part)
        right[at : at + width] = high
        right[2 * width + at : 3 * width + at] = middle
        right[4 * width + at : 5 * width + at] = high
    solve[...] = six_right(square.T)


def couple(ids, inverse, panel, middles):
    width, span = panel.shape
    operands = [inverse, panel, *middles]
    shapes = [(6 * width, span), (6 * width, width)]
    return call(
        couple_kernel,
        ids,
        operands,
        [full(o.shape) for o in operands],
        [jax.ShapeDtypeStruct(s, jnp.bfloat16) for s in shapes],
        [full(s) for s in shapes],
        12 * (2 * width**3 + 2 * width * width * span),
    )


def update_kernel(count, ids, trailing, basis_high, basis_middle, right, solve, *refs):
    pieces, (out, piece, left) = refs[: max(2, count)], refs[-3:]
    width = basis_high.shape[1]
    step = pl.program_id(0)
    for at in range(count):

        @pl.when(step == at)
        def _():
            if count > 1:
                piece[...] = pieces[at][...]
            else:
                piece[:4] = pieces[0][...]
                piece[4:] = pieces[1][...]

    rows = times(six_left(piece[...].reshape(-1, width)), solve[...])
    rows_high, rows_middle, _ = thirds(rows)
    parts = ((0, basis_high[...], basis_middle[...]), (width, rows_high, rows_middle))
    for at, high, middle in parts:
        left[:, at : at + width] = high
        left[:, 2 * width + at : 3 * width + at] = high
        left[:, 4 * width + at : 5 * width + at] = middle
    out[...] = trailing[...] - times(left[...], right[...])


def update(ids, trailing, basis, right, solve, pieces, out):
    n, width = pieces[0][0].shape[1:]
    span, count = trailing.shape[1], len(pieces)
    if out is None:
        at = lambda i, ids: (lax.rem(ids[3] + lax.rem(3 * i, 5), 4), 0)
    else:
        at = lambda i, ids: (lax.rem(ids[3] + 2, 4), 0)
    block = pl.BlockSpec((8 * n, span), at)
    rest = [right, solve] + [half for piece in pieces for half in piece]
    operands = [trailing, *basis, *rest]
    in_specs = [block] + [pl.BlockSpec((8 * n, width), at)] * 2 + [full(o.shape) for o in rest]
    aliases = {}
    if out is not None:
        operands.append(out)
        in_specs.append(pl.BlockSpec(memory_space=pl.ANY))
        aliases = {len(operands): 0}
    return call(
        functools.partial(update_kernel, count),
        ids,
        operands,
        in_specs,
        f32(*trailing.shape),
        block,
        6 * count * 8 * n * 2 * width * span,
        aliases,
        [pltpu.VMEM((8, n, width), jnp.float32), pltpu.VMEM((8 * n, 6 * width), jnp.bfloat16)],
        count,
        UPDATE_GRANT,
    )


def shards(panel, trailing, vectors):
    n, width = panel.shape
    slab = width // 8
    ids = jnp.stack([lax.axis_index(a) for a in EVERYWHERE]).astype(jnp.int32)
    by_cols = [(c * 8 + r, r * 32 + c) for r in range(8) for c in range(32)]
    turn = [
        (device(y, core, z, x), device(z // 2, z % 2, 2 * y + core, x))
        for y in range(4)
        for core in range(2)
        for z in range(8)
        for x in range(4)
    ]

    moved = lax.ppermute(panel, EVERYWHERE, by_cols)
    first, second, copies = arrange(ids, gather_z(panel), moved)
    own, high, far, low = gather_x(first, second)
    columns = all_to_row(copies)
    cut = trailing.reshape(8, 4, n, -1)
    product, gram, rows = absorb(ids, cut, [own, low, high])
    keep, send, rows = pack(ids, cut, far, product, gram, rows, columns, vectors.T)
    rows = rows.reshape(-1, width)

    *routed, rest = route(ids, keep, swap_core(send), n + slab)
    parts = [routed[0]] + [shift(routed[step], "y", step) for step in (1, 2, 3)]
    own_product, middle = settle(ids, parts, n)
    turned = lax.ppermute(own_product, EVERYWHERE, turn)
    parts = [middle] + [shift(middle, "x", step) for step in (1, 2, 3)]
    rest = rest + sum(shift(rest, "y", step) for step in (1, 2, 3))
    other_rest = swap_core(rest)
    blocks = lax.all_to_all(spread(ids, turned, parts), "z", 0, 0)
    upper, inverse, turns = factor(ids, rest, other_rest)
    panel_cols, high, low, rotated = finish(ids, inverse, columns, turns, vectors.T, rows)
    basis = [high, low]
    own, joined = split(ids, blocks, own_product, inverse)
    low, high = shift(own, "x", 1), shift(own, "x", -1)
    far = (shift(low[:4], "x", 1), shift(high[4:], "x", -1))
    right, solve = couple(ids, inverse, panel_cols, gather_row(joined))
    updated = update(ids, trailing, basis, right, solve, [(own,), (low,), (high,)], None)
    updated = update(ids, trailing, basis, right, solve, [far], updated)
    return (upper, updated, rotated.T)


def solution(mesh):
    fine = Mesh(mesh.devices.reshape(4, 2, 8, 4), EVERYWHERE)
    row, col = ("y", "core"), ("z", "x")
    return jax.shard_map(
        shards,
        mesh=fine,
        in_specs=(P(row + col, None), P(row, col), P(row, col)),
        out_specs=(P(), P(row, col), P(row, col)),
        check_vma=False,
    )
```
